512 devices in a mesh: rows: 64 (over x, y, core), grp: 8 (over z).
Axes of the slice: x: 4, y: 8, z: 8, core: 2. Of those that a mesh axis runs over, the one named last changes fastest.
Arguments:
- a_blocks: bfloat16 [24576, 64, 512], P(('rows', 'grp')), may hold values from -1 to 1
- prolong: bfloat16 [24576, 64, 128], P(('rows', 'grp')), may hold values from -1 to 1
- a_cols: int32 [24576, 8], P(('rows', 'grp')), may hold values from -1 to 55, as said below
- read_slots: int32 [1024, 4], P(('rows', 'grp')), may hold values from -1 to 47, as said below
- agg: int32 [24576], P(('rows', 'grp')), may hold values from 0 to 7
- rap_slot: int32 [24576, 8], P(('rows', 'grp')), may hold values from 0 to 7
Outputs:
- coarse_op: float32 [512, 8, 16384], P(('rows', 'grp'))
The draws below stay inside these ranges and needn't reach their ends.
Inputs may be any that keep to these rules, and one draw needn't show every extreme that they name: `a_cols`: slot 0 of every row is the row itself; an entry of 48 or more names a read-list entry that is not -1. `read_slots`: the entries of one list that are not -1 come first and are distinct; devices at the ends of rows have only -1 toward the missing side.
All inputs are finite; a program needn't handle non-finite values.
Results may differ from the reference program's by a relative error of at most 0.009.
Values may be sent and summed in bfloat16 or wider, within the bound.
A program may use at most 128 MiB of HBM per device.

```python
import jax
import jax.numpy as jnp
from jax import lax

BLOCK = 64
CWIDTH = 128
KSLOT = 8
CSLOT = 8
FB_DEV = 48
CAP = 4
NC_DEV = 1
NB = 24576
N_ROWS = 64
N_GRP = 8


def pattern_draw(key):
    device_count = N_ROWS * N_GRP
    count_key, shuffle_key, local_key, pad_key = jax.random.split(key, 4)
    device_ids = jnp.arange(device_count, dtype=jnp.int32)
    row_place = device_ids // N_GRP
    counts = jax.random.randint(count_key, (device_count, 2), 1, CAP + 1)
    counts = jnp.where((device_ids % 3 == 0)[:, None], CAP, counts)
    counts = counts.at[:, 0].set(jnp.where(row_place == 0, 0, counts[:, 0]))
    counts = counts.at[:, 1].set(jnp.where(row_place == N_ROWS - 1, 0, counts[:, 1]))
    shuffle_keys = jax.random.split(shuffle_key, device_count * 2)
    shuffled = jax.vmap(lambda one_key: jax.random.permutation(one_key, FB_DEV))(shuffle_keys)
    first_col = shuffled[:, :1]
    shuffled = jnp.where(shuffled == FB_DEV - 1, first_col, shuffled)
    shuffled = shuffled.at[:, 0].set(FB_DEV - 1)
    read_table = shuffled[:, :CAP].reshape(device_count, 2, CAP)
    cap_ids = jnp.arange(CAP, dtype=jnp.int32)
    read_table = jnp.where(cap_ids[None, None, :] < counts[:, :, None], read_table, -1)
    local_cols = jax.random.randint(local_key, (device_count, FB_DEV, KSLOT), 0, FB_DEV)
    local_rows = jnp.arange(FB_DEV, dtype=jnp.int32)
    direction = jnp.minimum(local_rows // CAP, 1)
    within = local_rows % CAP
    usable = (local_rows < 2 * CAP)[None, :] & (within[None, :] < counts[:, direction])
    second = jnp.where(usable, FB_DEV + local_rows[None, :], local_cols[:, :, 1])
    pad_level = jax.random.randint(pad_key, (device_count,), 0, 4)
    pad_level = jnp.where(device_ids % 2 == 0, 3, pad_level)
    padded = jax.random.randint(jax.random.fold_in(pad_key, 1), (device_count, FB_DEV, KSLOT), 0, 8) < pad_level[:, None, None]
    slot_ids = jnp.arange(KSLOT, dtype=jnp.int32)
    padded = padded & (slot_ids >= 2)[None, None, :] | (slot_ids == KSLOT - 1)[None, None, :] & (pad_level > 0)[:, None, None]
    col_table = jnp.where(padded, -1, local_cols)
    col_table = col_table.at[:, :, 1].set(second)
    col_table = col_table.at[:, :, 0].set(jnp.broadcast_to(local_rows[None, :], (device_count, FB_DEV)))
    return (read_table.reshape(device_count * 2, CAP).astype(jnp.int32), col_table.reshape(device_count * FB_DEV, KSLOT).astype(jnp.int32))


def draw_a_cols(key, part):
    shared = pattern_draw(key)
    return shared[1]


def draw_read_slots(key, part):
    shared = pattern_draw(key)
    return shared[0]


def draw_agg(key, part):
    key = jax.random.fold_in(key, 5)
    own_key, stray_key, pick_key = jax.random.split(key, 3)
    total_rows = FB_DEV * N_ROWS * N_GRP
    group_place = jnp.arange(total_rows, dtype=jnp.int32) // FB_DEV % N_GRP
    own = group_place * NC_DEV + jax.random.randint(own_key, (total_rows,), 0, NC_DEV)
    stray = jax.random.randint(stray_key, (total_rows,), 0, NC_DEV * N_GRP)
    chosen = jax.random.randint(pick_key, (total_rows,), 0, 4) == 0
    return jnp.where(chosen, stray, own).astype(jnp.int32)


def draw_rap_slot(key, part):
    key = jax.random.fold_in(key, 7)
    return jax.random.randint(key, (FB_DEV * N_ROWS * N_GRP, KSLOT), 0, CSLOT).astype(jnp.int32)


def level_of(rng, dims, cuts, least, high):
    factor_of = 1.0
    for position, shards_of in cuts:
        draws = jax.random.uniform(jax.random.fold_in(jax.random.fold_in(rng, 6), position), (shards_of,), jnp.float32, least / len(cuts), high / len(cuts))
        factor_of = factor_of * jnp.repeat(jnp.exp(draws), dims[position] // shards_of).reshape((-1,) + (1,) * (len(dims) - 1 - position))
    return factor_of


def centred(key, shape, spread, bound, cuts=(), held_as=jnp.bfloat16):
    level = level_of(key, shape, cuts, -0.22, 0.18) if cuts else 1.0
    drawn = jax.random.normal(key, shape, jnp.float32) * spread * level
    return jnp.minimum(jnp.maximum(drawn, -bound), bound).astype(held_as)


def setup_inputs(seed: int = 0) -> dict:
    key_list = jax.random.split(jax.random.key(seed), 7)
    return {
        "a_blocks": centred(key_list[0], (NB, BLOCK, KSLOT * BLOCK), 0.125, 1.0, ((0, 512),)),
        "prolong": centred(key_list[1], (NB, BLOCK, CWIDTH), 0.125, 1.0, ((0, 512),)),
        "a_cols": draw_a_cols(jax.random.fold_in(key_list[6], 71), 0),
        "read_slots": draw_read_slots(jax.random.fold_in(key_list[6], 71), 0),
        "agg": draw_agg(jax.random.fold_in(key_list[6], 71), 0),
        "rap_slot": draw_rap_slot(jax.random.fold_in(key_list[6], 71), 0),
    }


def reference(a_blocks, prolong, a_cols, read_slots, agg, rap_slot):
    device_count = N_ROWS * N_GRP
    device_ids = jnp.arange(device_count, dtype=jnp.int32)
    read_table = read_slots.reshape(device_count, 2, CAP)
    lower_owner = jnp.clip(device_ids - N_GRP, 0, device_count - 1)
    upper_owner = jnp.clip(device_ids + N_GRP, 0, device_count - 1)
    local_glob = device_ids[:, None] * FB_DEV + jnp.arange(FB_DEV, dtype=jnp.int32)[None, :]
    lower_glob = lower_owner[:, None] * FB_DEV + jnp.maximum(read_table[:, 0], 0)
    upper_glob = upper_owner[:, None] * FB_DEV + jnp.maximum(read_table[:, 1], 0)
    col_lookup = jnp.concatenate([local_glob, lower_glob, upper_glob], axis=1).astype(jnp.int32)
    col_table = a_cols.reshape(device_count, FB_DEV * KSLOT)
    col_index = jnp.take_along_axis(col_lookup, jnp.maximum(col_table, 0), axis=1)
    col_index = col_index.reshape(device_count * FB_DEV, KSLOT).astype(jnp.int32)
    panel_rows = NC_DEV * N_GRP

    def one_device(device):
        start = (device * FB_DEV).astype(jnp.int32)
        blocks = lax.dynamic_slice_in_dim(a_blocks, start, FB_DEV, 0)
        blocks = blocks.reshape(FB_DEV, BLOCK, KSLOT, BLOCK).astype(jnp.float32)
        own_p = lax.dynamic_slice_in_dim(prolong, start, FB_DEV, 0).astype(jnp.float32)
        cols_here = lax.dynamic_slice_in_dim(col_index, start, FB_DEV, 0)
        live = lax.dynamic_slice_in_dim(a_cols, start, FB_DEV, 0) >= 0
        gathered = prolong[cols_here].astype(jnp.float32)
        near = jnp.einsum("iakb,ikbc->ikac", blocks, gathered)
        near = jnp.where(live[:, :, None, None], near, 0.0).astype(jnp.bfloat16)
        terms = jnp.einsum("ibd,ikbc->ikdc", own_p, near.astype(jnp.float32))
        terms = jnp.where(live[:, :, None, None], terms, 0.0)
        aggs = lax.dynamic_slice_in_dim(agg, start, FB_DEV, 0)
        slots_here = lax.dynamic_slice_in_dim(rap_slot, start, FB_DEV, 0)
        target = (aggs[:, None] * CSLOT + slots_here).reshape(-1)
        partial_value = jax.ops.segment_sum(terms.reshape(FB_DEV * KSLOT, CWIDTH * CWIDTH), target, num_segments=panel_rows * CSLOT)
        return partial_value.astype(jnp.bfloat16)

    def one_group(group):
        total = jnp.zeros((panel_rows * CSLOT, CWIDTH * CWIDTH), jnp.float32)
        for member in range(N_GRP):
            total = total + one_device(group * N_GRP + member).astype(jnp.float32)
        return total

    panels = lax.map(one_group, jnp.arange(N_ROWS, dtype=jnp.int32))
    return panels.reshape(N_ROWS * panel_rows, CSLOT, CWIDTH * CWIDTH)
```

```python
import functools

import jax
import jax.numpy as jnp
from jax import lax
from jax.experimental import pallas as pl
from jax.experimental.pallas import tpu as pltpu
from jax.sharding import PartitionSpec as P

CSLOT = 8
MESH = pl.DeviceIdType.MESH


def lane_pair(left, right, rows):
    lanes = lax.broadcasted_iota(jnp.int32, (rows, 128), 1)
    return jnp.where(lanes < 64, left, right)


def indicator(value, wanted):
    return jnp.where(value == wanted, 1.0, 0.0).astype(jnp.bfloat16)


def kernel(
    row_count, grp_count,
    reads_ref, cols_ref, agg_ref, rap_ref, a_hbm, p_hbm,
    out_ref,
    a_v, p_loc, p_all, p_masked, spread, near, req_v, req_s, stage, outgoing, incoming,
    local_sem, req_send, req_recv, rep_send, rep_recv, ring_send, ring_recv,
):
    shard_rows, cells, _ = a_v.shape
    slot_count = cols_ref.shape[0]
    cap = stage.shape[1]
    half = grp_count // 2
    row, grp = lax.axis_index("rows"), lax.axis_index("grp")
    above, below = lax.rem(row + 1, row_count), lax.rem(row + row_count - 1, row_count)
    ahead, behind = lax.rem(grp + 1, grp_count), lax.rem(grp + grp_count - 1, grp_count)

    a_copy = pltpu.make_async_copy(a_hbm, a_v, local_sem.at[0])
    p_copy = pltpu.make_async_copy(p_hbm, p_loc, local_sem.at[1])
    all_copy = pltpu.make_async_copy(p_hbm, p_all.at[pl.ds(0, shard_rows)], local_sem.at[2])
    p_copy.start()
    a_copy.start()
    all_copy.start()

    barrier = pltpu.get_barrier_semaphore()
    for device in ({"rows": above}, {"rows": below}, {"grp": ahead}, {"grp": behind}):
        pl.semaphore_signal(barrier, inc=1, device_id=device, device_id_type=MESH)
    pl.semaphore_wait(barrier, 4)

    def request(side):
        return pltpu.make_async_remote_copy(
            src_ref=reads_ref,
            dst_ref=req_v.at[1 - side],
            send_sem=req_send.at[side],
            recv_sem=req_recv.at[1 - side],
            device_id={"rows": (below, above)[side]},
            device_id_type=MESH,
        )

    def reply(side):
        return pltpu.make_async_remote_copy(
            src_ref=stage.at[side],
            dst_ref=p_all.at[pl.ds(shard_rows + (1 - side) * cap, cap)],
            send_sem=rep_send.at[side],
            recv_sem=rep_recv.at[1 - side],
            device_id={"rows": (below, above)[side]},
            device_id_type=MESH,
        )

    for side in (0, 1):
        request(side).start()

    p_copy.wait()

    @pl.loop(0, shard_rows // 2)
    def _(pair):
        block = p_loc[pl.ds(pair * 2, 2)].reshape(128, 128).T
        owner = lane_pair(agg_ref[pair * 2], agg_ref[pair * 2 + 1], 16)
        lanes = pl.ds(pl.multiple_of(pair * 128, 128), 128)
        for q in range(grp_count):
            keep = indicator(owner, q)
            p_masked[q, :, lanes] = block * jnp.concatenate([keep] * 8, axis=0)

    for side in (0, 1):
        request(side).wait()
    req_copy = pltpu.make_async_copy(req_v, req_s, local_sem.at[3])
    req_copy.start()
    req_copy.wait()
    for side in (0, 1):
        for c in range(cap):
            stage[side, c] = p_loc[jnp.maximum(req_s[side, 1 - side, c], 0)]
        reply(side).start()

    a_copy.wait()

    @pl.loop(0, shard_rows)
    def _(i):
        places = [
            jnp.where(cols_ref[k, i] >= 0, rap_ref[k, i], -1) for k in range(slot_count)
        ]
        for k in range(0, slot_count, 2):
            lanes = pl.ds(k * cells, 2 * cells)
            block = a_v[i, :, lanes]
            place = lane_pair(places[k], places[k + 1], 16)
            for s in range(CSLOT):
                keep = indicator(place, s)
                spread[i, pl.ds(s * cells, cells), lanes] = block * jnp.concatenate(
                    [keep] * (cells // 16), axis=0
                )

    all_copy.wait()
    for side in (0, 1):
        reply(side).wait()

    @pl.loop(0, shard_rows)
    def _(i):
        columns = jnp.concatenate(
            [p_all[jnp.maximum(cols_ref[k, i], 0)] for k in range(slot_count)], axis=0
        )
        product = jnp.dot(spread[i], columns, preferred_element_type=jnp.float32)
        product = product.astype(jnp.bfloat16)
        rows = pl.ds(pl.multiple_of(i * cells, cells), cells)
        for s in range(CSLOT):
            near[s // 2, rows, (s % 2) * 128 : (s % 2 + 1) * 128] = product[
                s * cells : (s + 1) * cells
            ]

    def hop(way, step, s):
        return pltpu.make_async_remote_copy(
            src_ref=outgoing.at[way, step, s],
            dst_ref=incoming.at[way, step, s],
            send_sem=ring_send.at[way, step, s],
            recv_sem=ring_recv.at[way, step, s],
            device_id={"grp": (ahead, behind)[way]},
            device_id_type=MESH,
        )

    def own_terms(q, pair):
        return jnp.dot(p_masked[q], near[pair], preferred_element_type=jnp.float32)

    def forward(way, step, pair, receives):
        away = half - step
        q = lax.rem(grp + (away if way == 0 else grp_count - away), grp_count)
        terms = own_terms(q, pair)
        for h in (0, 1):
            s = pair * 2 + h
            total = terms[:, h * 128 : (h + 1) * 128]
            if receives:
                hop(way, step - 1, s).wait_recv()
                total = total + incoming[way, step - 1, s].astype(jnp.float32)
            outgoing[way, step, s] = total.astype(jnp.bfloat16)
            hop(way, step, s).start()

    @pl.loop(0, 2)
    def _(j):
        forward(0, 0, j, False)
        forward(1, 0, j + 2, False)

    @pl.loop(0, 2)
    def _(j):
        forward(0, 1, j + 2, False)
        forward(1, 1, j, False)

    @pl.loop(2, 4 * (half - 1))
    def _(n):
        step, j = 1 + n // 4, n % 4
        forward(0, step, (j + 2) % 4, True)
        forward(1, step, j, True)

    @pl.loop(0, 4)
    def _(pair):
        terms = own_terms(grp, pair)
        for h in (0, 1):
            s = pair * 2 + h
            total = terms[:, h * 128 : (h + 1) * 128]
            for way in (0, 1):
                hop(way, half - 1, s).wait_recv()
                total = total + incoming[way, half - 1, s].astype(jnp.float32)
            out_ref[s] = total

    for way in (0, 1):
        @pl.loop(0, 4)
        def _(s, way=way):
            hop(way, 0, s + 4 * way).wait_send()

        @pl.loop(8, 8 * half)
        def _(n, way=way):
            hop(way, n // 8, n % 8).wait_send()


def on_device(row_count, grp_count, a_blocks, prolong, a_cols, read_slots, agg, rap_slot):
    shard_rows, cells, width = a_blocks.shape
    coarse = prolong.shape[2]
    cap = read_slots.shape[1]
    half = grp_count // 2
    vmem = pl.BlockSpec(memory_space=pltpu.VMEM)
    smem = pl.BlockSpec(memory_space=pltpu.SMEM)
    hbm = pl.BlockSpec(memory_space=pl.ANY)
    b16 = jnp.bfloat16
    dma = pltpu.SemaphoreType.DMA
    out = pl.pallas_call(
        functools.partial(kernel, row_count, grp_count),
        out_shape=jax.ShapeDtypeStruct((CSLOT, coarse, coarse), jnp.float32),
        in_specs=[vmem, smem, smem, smem, hbm, hbm],
        out_specs=vmem,
        scratch_shapes=[
            pltpu.VMEM((shard_rows, cells, width), b16),
            pltpu.VMEM((shard_rows, cells, coarse), b16),
            pltpu.VMEM((shard_rows + 2 * cap, cells, coarse), b16),
            pltpu.VMEM((grp_count, coarse, shard_rows * cells), b16),
            pltpu.VMEM((shard_rows, CSLOT * cells, width), b16),
            pltpu.VMEM((CSLOT // 2, shard_rows * cells, 2 * coarse), b16),
            pltpu.VMEM((2, 2, cap), jnp.int32),
            pltpu.SMEM((2, 2, cap), jnp.int32),
            pltpu.VMEM((2, cap, cells, coarse), b16),
            pltpu.VMEM((2, half, CSLOT, coarse, coarse), b16),
            pltpu.VMEM((2, half, CSLOT, coarse, coarse), b16),
            dma((4,)),
            dma((2,)),
            dma((2,)),
            dma((2,)),
            dma((2,)),
            dma((2, half, CSLOT)),
            dma((2, half, CSLOT)),
        ],
        compiler_params=pltpu.CompilerParams(
            collective_id=0, has_side_effects=True, vmem_limit_bytes=58 * 1024 * 1024
        ),
    )(read_slots, a_cols.T, agg, rap_slot.T, a_blocks, prolong)
    return out.reshape(1, CSLOT, coarse * coarse)


def solution(mesh):
    return jax.shard_map(
        functools.partial(on_device, mesh.shape["rows"], mesh.shape["grp"]),
        mesh=mesh,
        in_specs=(
            P(("rows", "grp"), None, None),
            P(("rows", "grp"), None, None),
            P(("rows", "grp"), None),
            P(("rows", "grp"), None),
            P(("rows", "grp")),
            P(("rows", "grp"), None),
        ),
        out_specs=P(("rows", "grp"), None, None),
        check_vma=False,
    )
```

```python
import functools

import jax
import jax.numpy as jnp
from jax import lax
from jax.experimental import pallas as pl
from jax.experimental.pallas import tpu as pltpu
from jax.sharding import PartitionSpec as P

CSLOT = 8
MESH = pl.DeviceIdType.MESH


def lane_pair(left, right, rows):
    lanes = lax.broadcasted_iota(jnp.int32, (rows, 128), 1)
    return jnp.where(lanes < 64, left, right)


def indicator(value, wanted):
    return jnp.where(value == wanted, 1.0, 0.0).astype(jnp.bfloat16)


def kernel(
    row_count, grp_count,
    reads_ref, cols_ref, agg_ref, rap_ref, a_hbm, p_hbm,
    out_ref,
    a_v, p_loc, p_all, p_turned, p_masked, near, total_v, req_v, req_s, stage, outgoing, incoming,
    local_sem, req_send, req_recv, rep_send, rep_recv, ring_send, ring_recv,
):
    shard_rows, cells, _ = a_v.shape
    slot_count = cols_ref.shape[0]
    cap = stage.shape[1]
    half = grp_count // 2
    row, grp = lax.axis_index("rows"), lax.axis_index("grp")
    above, below = lax.rem(row + 1, row_count), lax.rem(row + row_count - 1, row_count)
    ahead, behind = lax.rem(grp + 1, grp_count), lax.rem(grp + grp_count - 1, grp_count)

    a_copy = pltpu.make_async_copy(a_hbm, a_v, local_sem.at[0])
    p_copy = pltpu.make_async_copy(p_hbm, p_loc, local_sem.at[1])
    all_copy = pltpu.make_async_copy(p_hbm, p_all.at[pl.ds(0, shard_rows)], local_sem.at[2])
    p_copy.start()
    a_copy.start()
    all_copy.start()

    barrier = pltpu.get_barrier_semaphore()
    for device in ({"rows": above}, {"rows": below}, {"grp": ahead}, {"grp": behind}):
        pl.semaphore_signal(barrier, inc=1, device_id=device, device_id_type=MESH)
    pl.semaphore_wait(barrier, 4)

    def request(side):
        return pltpu.make_async_remote_copy(
            src_ref=reads_ref,
            dst_ref=req_v.at[1 - side],
            send_sem=req_send.at[side],
            recv_sem=req_recv.at[1 - side],
            device_id={"rows": (below, above)[side]},
            device_id_type=MESH,
        )

    def reply(side):
        return pltpu.make_async_remote_copy(
            src_ref=stage.at[side],
            dst_ref=p_all.at[pl.ds(shard_rows + (1 - side) * cap, cap)],
            send_sem=rep_send.at[side],
            recv_sem=rep_recv.at[1 - side],
            device_id={"rows": (below, above)[side]},
            device_id_type=MESH,
        )

    for side in (0, 1):
        request(side).start()

    p_copy.wait()

    @pl.loop(0, shard_rows // 2, unroll=4)
    def _(pair):
        lanes = pl.ds(pl.multiple_of(pair * 128, 128), 128)
        p_turned[:, lanes] = p_loc[pl.ds(pair * 2, 2)].reshape(128, 128).T

    for side in (0, 1):
        request(side).wait()
    req_copy = pltpu.make_async_copy(req_v, req_s, local_sem.at[3])
    req_copy.start()
    req_copy.wait()
    for side in (0, 1):
        for c in range(cap):
            stage[side, c] = p_loc[jnp.maximum(req_s[side, 1 - side, c], 0)]
        reply(side).start()

    @pl.loop(0, shard_rows // 2)
    def _(pair):
        lanes = pl.ds(pl.multiple_of(pair * 128, 128), 128)
        block = p_turned[:, lanes]
        owner = lane_pair(agg_ref[pair * 2], agg_ref[pair * 2 + 1], 16)
        for q in range(grp_count):
            keep = indicator(owner, q)
            p_masked[q, :, lanes] = block * jnp.concatenate([keep] * 8, axis=0)

    a_copy.wait()
    all_copy.wait()
    for side in (0, 1):
        reply(side).wait()

    @pl.loop(0, shard_rows, unroll=4)
    def _(i):
        columns = jnp.concatenate(
            [p_all[jnp.maximum(cols_ref[k, i], 0)] for k in range(slot_count)], axis=0
        )
        places = [
            jnp.where(cols_ref[k, i] >= 0, rap_ref[k, i], -1) for k in range(slot_count)
        ]
        spread = []
        for k in range(0, slot_count, 2):
            block = a_v[i, :, k * cells : (k + 2) * cells]
            place = lane_pair(places[k], places[k + 1], 16)
            keeps = [indicator(place, s) for s in range(CSLOT)]
            spread.append(
                jnp.concatenate(
                    [block * jnp.concatenate([keep] * (cells // 16), axis=0) for keep in keeps],
                    axis=0,
                )
            )
        product = jnp.dot(
            jnp.concatenate(spread, axis=1), columns, preferred_element_type=jnp.float32
        ).astype(jnp.bfloat16)
        rows = pl.ds(pl.multiple_of(i * cells, cells), cells)
        for s in range(CSLOT):
            near[s // 2, rows, (s % 2) * 128 : (s % 2 + 1) * 128] = product[
                s * cells : (s + 1) * cells
            ]

    def hop(way, step, s):
        return pltpu.make_async_remote_copy(
            src_ref=outgoing.at[way, step, s],
            dst_ref=incoming.at[way, step, s],
            send_sem=ring_send.at[way, step, s],
            recv_sem=ring_recv.at[way, step, s],
            device_id={"grp": (ahead, behind)[way]},
            device_id_type=MESH,
        )

    def own_terms(first, second, pair):
        left = jnp.concatenate([p_masked[first], p_masked[second]], axis=0)
        return jnp.dot(left, near[pair], preferred_element_type=jnp.float32)

    def forward(way, step, pair, terms, receives):
        for h in (0, 1):
            s = pair * 2 + h
            total = terms[way * 128 : (way + 1) * 128, h * 128 : (h + 1) * 128]
            if receives:
                hop(way, step - 1, s).wait_recv()
                total = total + incoming[way, step - 1, s].astype(jnp.float32)
            outgoing[way, step, s] = total.astype(jnp.bfloat16)
            hop(way, step, s).start()

    def both(step, pair):
        away = half - step
        return own_terms(
            lax.rem(grp + away, grp_count), lax.rem(grp + grp_count - away, grp_count), pair
        )

    @pl.loop(0, 2)
    def _(j):
        for pair, way in ((j, 0), (j + 2, 1)):
            terms = own_terms(lax.rem(grp + half, grp_count), grp, pair)
            for h in (0, 1):
                s = pair * 2 + h
                lanes = slice(h * 128, (h + 1) * 128)
                outgoing[way, 0, s] = terms[:128, lanes].astype(jnp.bfloat16)
                hop(way, 0, s).start()
                total_v[pl.ds(pl.multiple_of(s * 128, 128), 128)] = terms[128:, lanes]

    @pl.loop(0, 2)
    def _(j):
        for pair, fresh in ((j, 1), (j + 2, 0)):
            terms = both(1, pair)
            forward(fresh, 1, pair, terms, False)
            forward(1 - fresh, 1, pair, terms, True)

    @pl.loop(0, 4 * (half - 2))
    def _(n):
        step, pair = 2 + n // 4, (n % 4) // 2 + 2 * (n % 2)
        terms = both(step, pair)
        forward(0, step, pair, terms, True)
        forward(1, step, pair, terms, True)

    for way in (0, 1):
        @pl.loop(0, 4)
        def _(s, way=way):
            hop(way, 0, s + 4 * way).wait_send()

        @pl.loop(8, 8 * (half - 1))
        def _(n, way=way):
            hop(way, n // 8, n % 8).wait_send()

    @pl.loop(0, 8)
    def _(n):
        s = 4 * ((n // 2) % 2) + 2 * (n // 4) + n % 2
        rows = pl.ds(pl.multiple_of(s * 128, 128), 128)
        total = total_v[rows]
        for way in (0, 1):
            hop(way, half - 1, s).wait_recv()
            total = total + incoming[way, half - 1, s].astype(jnp.float32)
        total_v[rows] = total

    for d in range(128):
        out_ref[0, :, d * 128 : (d + 1) * 128] = total_v[pl.ds(d, CSLOT, stride=128)]

    for way in (0, 1):
        @pl.loop(0, 8)
        def _(s, way=way):
            hop(way, half - 1, s).wait_send()


def on_device(row_count, grp_count, a_blocks, prolong, a_cols, read_slots, agg, rap_slot):
    shard_rows, cells, width = a_blocks.shape
    coarse = prolong.shape[2]
    cap = read_slots.shape[1]
    half = grp_count // 2
    vmem = pl.BlockSpec(memory_space=pltpu.VMEM)
    smem = pl.BlockSpec(memory_space=pltpu.SMEM)
    hbm = pl.BlockSpec(memory_space=pl.ANY)
    b16 = jnp.bfloat16
    dma = pltpu.SemaphoreType.DMA
    return pl.pallas_call(
        functools.partial(kernel, row_count, grp_count),
        out_shape=jax.ShapeDtypeStruct((1, CSLOT, coarse * coarse), jnp.float32),
        in_specs=[vmem, smem, smem, smem, hbm, hbm],
        out_specs=vmem,
        scratch_shapes=[
            pltpu.VMEM((shard_rows, cells, width), b16),
            pltpu.VMEM((shard_rows, cells, coarse), b16),
            pltpu.VMEM((shard_rows + 2 * cap, cells, coarse), b16),
            pltpu.VMEM((coarse, shard_rows * cells), b16),
            pltpu.VMEM((grp_count, coarse, shard_rows * cells), b16),
            pltpu.VMEM((CSLOT // 2, shard_rows * cells, 2 * coarse), b16),
            pltpu.VMEM((CSLOT * coarse, coarse), jnp.float32),
            pltpu.VMEM((2, 2, cap), jnp.int32),
            pltpu.SMEM((2, 2, cap), jnp.int32),
            pltpu.VMEM((2, cap, cells, coarse), b16),
            pltpu.VMEM((2, half, CSLOT, coarse, coarse), b16),
            pltpu.VMEM((2, half, CSLOT, coarse, coarse), b16),
            dma((4,)),
            dma((2,)),
            dma((2,)),
            dma((2,)),
            dma((2,)),
            dma((2, half, CSLOT)),
            dma((2, half, CSLOT)),
        ],
        compiler_params=pltpu.CompilerParams(
            collective_id=0, has_side_effects=True, vmem_limit_bytes=56 * 1024 * 1024
        ),
    )(read_slots, a_cols.T, agg, rap_slot.T, a_blocks, prolong)


def solution(mesh):
    return jax.shard_map(
        functools.partial(on_device, mesh.shape["rows"], mesh.shape["grp"]),
        mesh=mesh,
        in_specs=(
            P(("rows", "grp"), None, None),
            P(("rows", "grp"), None, None),
            P(("rows", "grp"), None),
            P(("rows", "grp"), None),
            P(("rows", "grp")),
            P(("rows", "grp"), None),
        ),
        out_specs=P(("rows", "grp"), None, None),
        check_vma=False,
    )
```

```python
import functools

import jax
import jax.numpy as jnp
from jax import lax
from jax.experimental import pallas as pl
from jax.experimental.pallas import tpu as pltpu
from jax.sharding import PartitionSpec as P

CSLOT = 8
MESH = pl.DeviceIdType.MESH


def lane_pair(left, right, rows):
    lanes = lax.broadcasted_iota(jnp.int32, (rows, 128), 1)
    return jnp.where(lanes < 64, left, right)


def indicator(value, wanted):
    return jnp.where(value == wanted, 1.0, 0.0).astype(jnp.bfloat16)


def kernel(
    row_count, grp_count,
    reads_hbm, cols_hbm, agg_hbm, rap_hbm, a_hbm, p_hbm,
    out_ref,
    cols_ref, agg_ref, rap_ref,
    a_v, p_loc, p_all, p_turned, p_masked, near, total_v, req_v, req_s, stage, outgoing, incoming,
    local_sem, req_send, req_recv, rep_send, rep_recv, ring_send, ring_recv,
):
    shard_rows, cells, _ = a_v.shape
    slot_count = cols_ref.shape[0]
    cap = stage.shape[1]
    half = grp_count // 2
    row, grp = lax.axis_index("rows"), lax.axis_index("grp")
    above, below = lax.rem(row + 1, row_count), lax.rem(row + row_count - 1, row_count)
    ahead, behind = lax.rem(grp + 1, grp_count), lax.rem(grp + grp_count - 1, grp_count)

    a_copy = pltpu.make_async_copy(a_hbm, a_v, local_sem.at[0])
    p_copy = pltpu.make_async_copy(p_hbm, p_loc, local_sem.at[1])
    all_copy = pltpu.make_async_copy(p_hbm, p_all.at[pl.ds(0, shard_rows)], local_sem.at[2])
    p_copy.start()
    a_copy.start()
    all_copy.start()
    index_copies = [
        pltpu.make_async_copy(source, target, local_sem.at[4 + n])
        for n, (source, target) in enumerate(
            ((agg_hbm, agg_ref), (cols_hbm, cols_ref), (rap_hbm, rap_ref))
        )
    ]
    for copy in index_copies:
        copy.start()

    barrier = pltpu.get_barrier_semaphore()
    for device in ({"rows": above}, {"rows": below}, {"grp": ahead}, {"grp": behind}):
        pl.semaphore_signal(barrier, inc=1, device_id=device, device_id_type=MESH)
    pl.semaphore_wait(barrier, 4)

    def request(side):
        return pltpu.make_async_remote_copy(
            src_ref=reads_hbm,
            dst_ref=req_v.at[1 - side],
            send_sem=req_send.at[side],
            recv_sem=req_recv.at[1 - side],
            device_id={"rows": (below, above)[side]},
            device_id_type=MESH,
        )

    def reply(side):
        return pltpu.make_async_remote_copy(
            src_ref=stage.at[side],
            dst_ref=p_all.at[pl.ds(shard_rows + (1 - side) * cap, cap)],
            send_sem=rep_send.at[side],
            recv_sem=rep_recv.at[1 - side],
            device_id={"rows": (below, above)[side]},
            device_id_type=MESH,
        )

    for side in (0, 1):
        request(side).start()

    p_copy.wait()

    @pl.loop(0, shard_rows // 2, unroll=4)
    def _(pair):
        lanes = pl.ds(pl.multiple_of(pair * 128, 128), 128)
        p_turned[:, lanes] = p_loc[pl.ds(pair * 2, 2)].reshape(128, 128).T

    for side in (0, 1):
        request(side).wait()
    req_copy = pltpu.make_async_copy(req_v, req_s, local_sem.at[3])
    req_copy.start()
    req_copy.wait()
    for side in (0, 1):
        for c in range(cap):
            stage[side, c] = p_loc[jnp.maximum(req_s[side, 1 - side, c], 0)]
        reply(side).start()

    for copy in index_copies:
        copy.wait()

    @pl.loop(0, shard_rows // 2)
    def _(pair):
        lanes = pl.ds(pl.multiple_of(pair * 128, 128), 128)
        block = p_turned[:, lanes]
        owner = lane_pair(agg_ref[pair * 2], agg_ref[pair * 2 + 1], 16)
        for q in range(grp_count):
            keep = indicator(owner, q)
            p_masked[q, :, lanes] = block * jnp.concatenate([keep] * 8, axis=0)

    a_copy.wait()
    all_copy.wait()
    for side in (0, 1):
        reply(side).wait()

    def slot_sums(i, slots):
        columns = jnp.concatenate(
            [p_all[jnp.maximum(cols_ref[k, i], 0)] for k in range(slot_count)], axis=0
        )
        places = [
            jnp.where(cols_ref[k, i] >= 0, rap_ref[k, i], -1) for k in range(slot_count)
        ]
        spread = []
        for k in range(0, slot_count, 2):
            block = a_v[i, :, k * cells : (k + 2) * cells]
            place = lane_pair(places[k], places[k + 1], 16)
            keeps = [indicator(place, s) for s in slots]
            spread.append(
                jnp.concatenate(
                    [block * jnp.concatenate([keep] * (cells // 16), axis=0) for keep in keeps],
                    axis=0,
                )
            )
        product = jnp.dot(
            jnp.concatenate(spread, axis=1), columns, preferred_element_type=jnp.float32
        ).astype(jnp.bfloat16)
        rows = pl.ds(pl.multiple_of(i * cells, cells), cells)
        for n, s in enumerate(slots):
            near[s // 2, rows, (s % 2) * 128 : (s % 2 + 1) * 128] = product[
                n * cells : (n + 1) * cells
            ]

    first_half, second_half = range(CSLOT // 2), range(CSLOT // 2, CSLOT)

    @pl.loop(0, shard_rows, unroll=4)
    def _(i):
        slot_sums(i, first_half)

    batch = shard_rows // 6

    def later_sums(n):
        @pl.loop(0, batch, unroll=min(4, batch))
        def _(j):
            slot_sums(n * batch + j, second_half)

    def hop(way, step, s):
        return pltpu.make_async_remote_copy(
            src_ref=outgoing.at[way, step, s],
            dst_ref=incoming.at[way, step, s],
            send_sem=ring_send.at[way, step, s],
            recv_sem=ring_recv.at[way, step, s],
            device_id={"grp": (ahead, behind)[way]},
            device_id_type=MESH,
        )

    def own_terms(first, second, pair):
        left = jnp.concatenate([p_masked[first], p_masked[second]], axis=0)
        return jnp.dot(left, near[pair], preferred_element_type=jnp.float32)

    def forward(way, step, pair, terms, receives):
        for h in (0, 1):
            s = pair * 2 + h
            total = terms[:, h * 128 : (h + 1) * 128]
            if receives:
                hop(way, step - 1, s).wait_recv()
                total = total + incoming[way, step - 1, s].astype(jnp.float32)
            outgoing[way, step, s] = total.astype(jnp.bfloat16)
            hop(way, step, s).start()

    def advance(long_way, step, pair):
        forth, back = half - step, grp_count - (half - 1 - step)
        if long_way == 1:
            forth, back = grp_count - forth, grp_count - back
        last = isinstance(step, int) and step == half - 1
        terms = own_terms(lax.rem(grp + forth, grp_count), lax.rem(grp + back, grp_count), pair)
        receives = not (isinstance(step, int) and step == 0)
        forward(long_way, step, pair, terms[:128], receives)
        if last:
            for h in (0, 1):
                rows = pl.ds(pl.multiple_of((pair * 2 + h) * 128, 128), 128)
                total_v[rows] = terms[128:, h * 128 : (h + 1) * 128]
        else:
            forward(1 - long_way, step, pair, terms[128:], receives)

    @pl.loop(0, 2)
    def _(n):
        advance(0, 0, n)
        later_sums(n)

    @pl.loop(0, 2 * (half - 2))
    def _(n):
        advance(0, 1 + n // 2, n % 2)
        if half > 2:
            later_sums(2 + n)

    for n in range(2 + 2 * (half - 2), 6):
        later_sums(n)

    @pl.loop(2, 4)
    def _(pair):
        advance(1, 0, pair)

    @pl.loop(0, 2)
    def _(pair):
        advance(0, half - 1, pair)

    @pl.loop(0, 2 * (half - 2))
    def _(n):
        advance(1, 1 + n // 2, 2 + n % 2)

    @pl.loop(2, 4)
    def _(pair):
        advance(1, half - 1, pair)

    def settle(way, long):
        @pl.loop(0, 4 * (half if long else half - 1))
        def _(n):
            hop(way, n // 4, n % 4 + (4 if (way == 1) == long else 0)).wait_send()

    settle(0, True)
    settle(0, False)
    settle(1, False)

    @pl.loop(0, CSLOT)
    def _(s):
        rows = pl.ds(pl.multiple_of(s * 128, 128), 128)
        total = total_v[rows]
        early = s // 4
        for way in (0, 1):
            step = half - 1 - (early if way == 0 else 1 - early)
            hop(way, step, s).wait_recv()
            total = total + incoming[way, step, s].astype(jnp.float32)
        total_v[rows] = total

    for d in range(128):
        out_ref[0, :, d * 128 : (d + 1) * 128] = total_v[pl.ds(d, CSLOT, stride=128)]

    settle(1, True)


def on_device(row_count, grp_count, a_blocks, prolong, a_cols, read_slots, agg, rap_slot):
    shard_rows, cells, width = a_blocks.shape
    coarse = prolong.shape[2]
    cap = read_slots.shape[1]
    half = grp_count // 2
    vmem = pl.BlockSpec(memory_space=pltpu.VMEM)
    hbm = pl.BlockSpec(memory_space=pltpu.HBM)
    b16 = jnp.bfloat16
    dma = pltpu.SemaphoreType.DMA
    return pl.pallas_call(
        functools.partial(kernel, row_count, grp_count),
        out_shape=jax.ShapeDtypeStruct((1, CSLOT, coarse * coarse), jnp.float32),
        in_specs=[hbm] * 6,
        out_specs=vmem,
        scratch_shapes=[
            pltpu.SMEM(a_cols.shape[::-1], jnp.int32),
            pltpu.SMEM(agg.shape, jnp.int32),
            pltpu.SMEM(rap_slot.shape[::-1], jnp.int32),
            pltpu.VMEM((shard_rows, cells, width), b16),
            pltpu.VMEM((shard_rows, cells, coarse), b16),
            pltpu.VMEM((shard_rows + 2 * cap, cells, coarse), b16),
            pltpu.VMEM((coarse, shard_rows * cells), b16),
            pltpu.VMEM((grp_count, coarse, shard_rows * cells), b16),
            pltpu.VMEM((CSLOT // 2, shard_rows * cells, 2 * coarse), b16),
            pltpu.VMEM((CSLOT * coarse, coarse), jnp.float32),
            pltpu.VMEM((2, 2, cap), jnp.int32),
            pltpu.SMEM((2, 2, cap), jnp.int32),
            pltpu.VMEM((2, cap, cells, coarse), b16),
            pltpu.VMEM((2, half, CSLOT, coarse, coarse), b16),
            pltpu.VMEM((2, half, CSLOT, coarse, coarse), b16),
            dma((7,)),
            dma((2,)),
            dma((2,)),
            dma((2,)),
            dma((2,)),
            dma((2, half, CSLOT)),
            dma((2, half, CSLOT)),
        ],
        compiler_params=pltpu.CompilerParams(
            collective_id=0, has_side_effects=True, vmem_limit_bytes=56 * 1024 * 1024
        ),
    )(read_slots, a_cols.T, agg, rap_slot.T, a_blocks, prolong)


def solution(mesh):
    return jax.shard_map(
        functools.partial(on_device, mesh.shape["rows"], mesh.shape["grp"]),
        mesh=mesh,
        in_specs=(
            P(("rows", "grp"), None, None),
            P(("rows", "grp"), None, None),
            P(("rows", "grp"), None),
            P(("rows", "grp"), None),
            P(("rows", "grp")),
            P(("rows", "grp"), None),
        ),
        out_specs=P(("rows", "grp"), None, None),
        check_vma=False,
    )
```

```python
import functools

import jax
import jax.numpy as jnp
from jax import lax
from jax.experimental import pallas as pl
from jax.experimental.pallas import tpu as pltpu
from jax.sharding import PartitionSpec as P

CSLOT = 8
MESH = pl.DeviceIdType.MESH


def lane_pair(left, right, rows):
    lanes = lax.broadcasted_iota(jnp.int32, (rows, 128), 1)
    return jnp.where(lanes < 64, left, right)


def indicator(value, wanted):
    return jnp.where(value == wanted, 1.0, 0.0).astype(jnp.bfloat16)


def kernel(
    row_count, grp_count,
    reads_hbm, cols_hbm, agg_hbm, rap_hbm, a_hbm, p_hbm,
    out_ref,
    cols_ref, agg_ref, rap_ref,
    a_v, p_loc, p_all, p_turned, p_masked, near, terms_v, total_v, req_v, req_s, stage, outgoing, incoming,
    local_sem, req_send, req_recv, rep_send, rep_recv, ring_send, ring_recv,
):
    shard_rows, cells, _ = a_v.shape
    slot_count = cols_ref.shape[0]
    cap = stage.shape[1]
    half = grp_count // 2
    row, grp = lax.axis_index("rows"), lax.axis_index("grp")
    above, below = lax.rem(row + 1, row_count), lax.rem(row + row_count - 1, row_count)
    ahead, behind = lax.rem(grp + 1, grp_count), lax.rem(grp + grp_count - 1, grp_count)

    a_copy = pltpu.make_async_copy(a_hbm, a_v, local_sem.at[0])
    p_copy = pltpu.make_async_copy(p_hbm, p_loc, local_sem.at[1])
    all_copy = pltpu.make_async_copy(p_hbm, p_all.at[pl.ds(0, shard_rows)], local_sem.at[2])
    p_copy.start()
    a_copy.start()
    all_copy.start()
    index_copies = [
        pltpu.make_async_copy(source, target, local_sem.at[4 + n])
        for n, (source, target) in enumerate(
            ((agg_hbm, agg_ref), (cols_hbm, cols_ref), (rap_hbm, rap_ref))
        )
    ]
    for copy in index_copies:
        copy.start()

    barrier = pltpu.get_barrier_semaphore()
    for device in ({"rows": above}, {"rows": below}, {"grp": ahead}, {"grp": behind}):
        pl.semaphore_signal(barrier, inc=1, device_id=device, device_id_type=MESH)
    pl.semaphore_wait(barrier, 4)

    def request(side):
        return pltpu.make_async_remote_copy(
            src_ref=reads_hbm,
            dst_ref=req_v.at[1 - side],
            send_sem=req_send.at[side],
            recv_sem=req_recv.at[1 - side],
            device_id={"rows": (below, above)[side]},
            device_id_type=MESH,
        )

    def reply(side):
        return pltpu.make_async_remote_copy(
            src_ref=stage.at[side],
            dst_ref=p_all.at[pl.ds(shard_rows + (1 - side) * cap, cap)],
            send_sem=rep_send.at[side],
            recv_sem=rep_recv.at[1 - side],
            device_id={"rows": (below, above)[side]},
            device_id_type=MESH,
        )

    for side in (0, 1):
        request(side).start()

    p_copy.wait()

    @pl.loop(0, shard_rows // 2, unroll=4)
    def _(pair):
        lanes = pl.ds(pl.multiple_of(pair * 128, 128), 128)
        p_turned[:, lanes] = p_loc[pl.ds(pair * 2, 2)].reshape(128, 128).T

    for side in (0, 1):
        request(side).wait()
    req_copy = pltpu.make_async_copy(req_v, req_s, local_sem.at[3])
    req_copy.start()
    req_copy.wait()
    for side in (0, 1):
        for c in range(cap):
            stage[side, c] = p_loc[jnp.maximum(req_s[side, 1 - side, c], 0)]
        reply(side).start()

    for copy in index_copies:
        copy.wait()

    @pl.loop(0, shard_rows // 2)
    def _(pair):
        lanes = pl.ds(pl.multiple_of(pair * 128, 128), 128)
        block = p_turned[:, lanes]
        owner = lane_pair(agg_ref[pair * 2], agg_ref[pair * 2 + 1], 16)
        for q in range(grp_count):
            keep = indicator(owner, q)
            p_masked[q, :, lanes] = block * jnp.concatenate([keep] * 8, axis=0)

    a_copy.wait()
    all_copy.wait()
    for side in (0, 1):
        reply(side).wait()

    def slot_sums(i, slots):
        columns = jnp.concatenate(
            [p_all[jnp.maximum(cols_ref[k, i], 0)] for k in range(slot_count)], axis=0
        )
        places = [
            jnp.where(cols_ref[k, i] >= 0, rap_ref[k, i], -1) for k in range(slot_count)
        ]
        spread = []
        for k in range(0, slot_count, 2):
            block = a_v[i, :, k * cells : (k + 2) * cells]
            place = lane_pair(places[k], places[k + 1], 16)
            keeps = [indicator(place, s) for s in slots]
            spread.append(
                jnp.concatenate(
                    [block * jnp.concatenate([keep] * (cells // 16), axis=0) for keep in keeps],
                    axis=0,
                )
            )
        product = jnp.dot(
            jnp.concatenate(spread, axis=1), columns, preferred_element_type=jnp.float32
        ).astype(jnp.bfloat16)
        rows = pl.ds(pl.multiple_of(i * cells, cells), cells)
        for n, s in enumerate(slots):
            near[s // 2, rows, (s % 2) * 128 : (s % 2 + 1) * 128] = product[
                n * cells : (n + 1) * cells
            ]

    first_half, second_half = range(CSLOT // 2), range(CSLOT // 2, CSLOT)

    @pl.loop(0, shard_rows, unroll=4)
    def _(i):
        slot_sums(i, first_half)

    def hop(way, step, part):
        return pltpu.make_async_remote_copy(
            src_ref=outgoing.at[way, step, part],
            dst_ref=incoming.at[way, step, part],
            send_sem=ring_send.at[way, step, part],
            recv_sem=ring_recv.at[way, step, part],
            device_id={"grp": (ahead, behind)[way]},
            device_id_type=MESH,
        )

    def advance(part, step, first=False, last=False):
        forth, back = half - step, grp_count - (half - 1 - step)
        if part == 1:
            forth, back = grp_count - forth, grp_count - back
        far, near_by = lax.rem(grp + forth, grp_count), lax.rem(grp + back, grp_count)

        @pl.loop(0, 2)
        def _(p):
            left = jnp.concatenate([p_masked[far], p_masked[near_by]], axis=0)
            terms_v[p] = jnp.dot(left, near[part * 2 + p], preferred_element_type=jnp.float32)

        def term(side, slot):
            lanes = slice(slot % 2 * 128, (slot % 2 + 1) * 128)
            return terms_v[slot // 2, side * 128 : (side + 1) * 128, lanes]

        for side, way in ((0, part), (1, 1 - part)):
            if last and side == 1:
                for slot in range(4):
                    total_v[pl.ds((part * 4 + slot) * 128, 128)] = term(side, slot)
                continue
            if not first:
                hop(way, step - 1, part).wait_recv()
            for slot in range(4):
                total = term(side, slot)
                if not first:
                    total = total + incoming[way, step - 1, part, slot].astype(jnp.float32)
                outgoing[way, step, part, slot] = total.astype(jnp.bfloat16)
            hop(way, step, part).start()

    advance(0, 0, first=True)

    @pl.loop(0, shard_rows, unroll=4)
    def _(i):
        slot_sums(i, second_half)

    advance(1, 0, first=True)

    @pl.loop(1, half - 1)
    def _(step):
        advance(0, step)
        advance(1, step)

    advance(0, half - 1, last=True)
    advance(1, half - 1, last=True)

    for step in range(half - 1):
        for way in (0, 1):
            for part in (0, 1):
                hop(way, step, part).wait_send()

    for part in (0, 1):
        hop(part, half - 1, part).wait_recv()
        hop(1 - part, half - 2, part).wait_recv()
        for slot in range(4):
            rows = pl.ds((part * 4 + slot) * 128, 128)
            total_v[rows] = (
                total_v[rows]
                + incoming[part, half - 1, part, slot].astype(jnp.float32)
                + incoming[1 - part, half - 2, part, slot].astype(jnp.float32)
            )

    for d in range(128):
        out_ref[0, :, d * 128 : (d + 1) * 128] = total_v[pl.ds(d, CSLOT, stride=128)]

    for part in (0, 1):
        hop(part, half - 1, part).wait_send()


def move(source, target, sems):
    width = source.shape[2] // 4
    copies = [
        pltpu.make_async_copy(
            source.at[:, :, pl.ds(n * width, width)], target.at[:, :, pl.ds(n * width, width)], sems.at[n]
        )
        for n in range(4)
    ]
    for copy in copies:
        copy.start()
    for copy in copies:
        copy.wait()


def on_device(row_count, grp_count, a_blocks, prolong, a_cols, read_slots, agg, rap_slot):
    shard_rows, cells, width = a_blocks.shape
    coarse = prolong.shape[2]
    cap = read_slots.shape[1]
    half = grp_count // 2
    vmem = pl.BlockSpec(memory_space=pltpu.VMEM)
    hbm = pl.BlockSpec(memory_space=pltpu.HBM)
    b16 = jnp.bfloat16
    dma = pltpu.SemaphoreType.DMA
    out = pl.pallas_call(
        functools.partial(kernel, row_count, grp_count),
        out_shape=jax.ShapeDtypeStruct((1, CSLOT, coarse * coarse), jnp.float32),
        in_specs=[hbm] * 6,
        out_specs=vmem,
        scratch_shapes=[
            pltpu.SMEM(a_cols.shape[::-1], jnp.int32),
            pltpu.SMEM(agg.shape, jnp.int32),
            pltpu.SMEM(rap_slot.shape[::-1], jnp.int32),
            pltpu.VMEM((shard_rows, cells, width), b16),
            pltpu.VMEM((shard_rows, cells, coarse), b16),
            pltpu.VMEM((shard_rows + 2 * cap, cells, coarse), b16),
            pltpu.VMEM((coarse, shard_rows * cells), b16),
            pltpu.VMEM((grp_count, coarse, shard_rows * cells), b16),
            pltpu.VMEM((CSLOT // 2, shard_rows * cells, 2 * coarse), b16),
            pltpu.VMEM((2, 2 * coarse, 2 * coarse), jnp.float32),
            pltpu.VMEM((CSLOT * coarse, coarse), jnp.float32),
            pltpu.VMEM((2, 2, cap), jnp.int32),
            pltpu.SMEM((2, 2, cap), jnp.int32),
            pltpu.VMEM((2, cap, cells, coarse), b16),
            pltpu.VMEM((2, half, 2, CSLOT // 2, coarse, coarse), b16),
            pltpu.VMEM((2, half, 2, CSLOT // 2, coarse, coarse), b16),
            dma((7,)),
            dma((2,)),
            dma((2,)),
            dma((2,)),
            dma((2,)),
            dma((2, half, 2)),
            dma((2, half, 2)),
        ],
        compiler_params=pltpu.CompilerParams(
            collective_id=0, has_side_effects=True, vmem_limit_bytes=56 * 1024 * 1024
        ),
    )(read_slots, a_cols.T, agg, rap_slot.T, a_blocks, prolong)
    return pl.pallas_call(
        move,
        out_shape=jax.ShapeDtypeStruct(out.shape, out.dtype),
        in_specs=[hbm],
        out_specs=hbm,
        scratch_shapes=[dma((4,))],
        compiler_params=pltpu.CompilerParams(vmem_limit_bytes=56 * 1024 * 1024),
    )(out)


def solution(mesh):
    return jax.shard_map(
        functools.partial(on_device, mesh.shape["rows"], mesh.shape["grp"]),
        mesh=mesh,
        in_specs=(
            P(("rows", "grp"), None, None),
            P(("rows", "grp"), None, None),
            P(("rows", "grp"), None),
            P(("rows", "grp"), None),
            P(("rows", "grp")),
            P(("rows", "grp"), None),
        ),
        out_specs=P(("rows", "grp"), None, None),
        check_vma=False,
    )
```

```python
import functools

import jax
import jax.numpy as jnp
from jax import lax
from jax.experimental import pallas as pl
from jax.experimental.pallas import tpu as pltpu
from jax.sharding import PartitionSpec as P

CSLOT = 8
MESH = pl.DeviceIdType.MESH


def lane_pair(left, right, rows):
    lanes = lax.broadcasted_iota(jnp.int32, (rows, 128), 1)
    return jnp.where(lanes < 64, left, right)


def indicator(value, wanted):
    return jnp.where(value == wanted, 1.0, 0.0).astype(jnp.bfloat16)


def kernel(
    row_count, grp_count,
    reads_hbm, cols_hbm, agg_hbm, rap_hbm, a_hbm, p_hbm,
    out_ref,
    cols_ref, agg_ref, rap_ref,
    a_v, p_loc, p_all, left, near, sums, order_v, order_s, keep_s, last_s, total_v, req_v, req_s, stage, outgoing, incoming,
    local_sem, req_send, req_recv, rep_send, rep_recv, ring_send, ring_recv,
):
    shard_rows, cells, _ = a_v.shape
    slot_count = cols_ref.shape[0]
    cap = stage.shape[1]
    half = grp_count // 2
    chunk_count = left.shape[0]
    row, grp = lax.axis_index("rows"), lax.axis_index("grp")
    above, below = lax.rem(row + 1, row_count), lax.rem(row + row_count - 1, row_count)
    ahead, behind = lax.rem(grp + 1, grp_count), lax.rem(grp + grp_count - 1, grp_count)

    a_copy = pltpu.make_async_copy(a_hbm, a_v, local_sem.at[0])
    p_copy = pltpu.make_async_copy(p_hbm, p_loc.at[pl.ds(0, shard_rows)], local_sem.at[1])
    all_copy = pltpu.make_async_copy(p_hbm, p_all.at[pl.ds(0, shard_rows)], local_sem.at[2])
    p_copy.start()
    a_copy.start()
    all_copy.start()
    index_copies = [
        pltpu.make_async_copy(source, target, local_sem.at[4 + n])
        for n, (source, target) in enumerate(
            ((agg_hbm, agg_ref), (cols_hbm, cols_ref), (rap_hbm, rap_ref))
        )
    ]
    for copy in index_copies:
        copy.start()

    barrier = pltpu.get_barrier_semaphore()
    for device in ({"rows": above}, {"rows": below}, {"grp": ahead}, {"grp": behind}):
        pl.semaphore_signal(barrier, inc=1, device_id=device, device_id_type=MESH)
    pl.semaphore_wait(barrier, 4)

    def request(side):
        return pltpu.make_async_remote_copy(
            src_ref=reads_hbm,
            dst_ref=req_v.at[1 - side],
            send_sem=req_send.at[side],
            recv_sem=req_recv.at[1 - side],
            device_id={"rows": (below, above)[side]},
            device_id_type=MESH,
        )

    def reply(side):
        return pltpu.make_async_remote_copy(
            src_ref=stage.at[side],
            dst_ref=p_all.at[pl.ds(shard_rows + (1 - side) * cap, cap)],
            send_sem=rep_send.at[side],
            recv_sem=rep_recv.at[1 - side],
            device_id={"rows": (below, above)[side]},
            device_id_type=MESH,
        )

    for side in (0, 1):
        request(side).start()

    p_copy.wait()
    p_loc[shard_rows] = jnp.zeros(p_loc.shape[1:], p_loc.dtype)
    for side in (0, 1):
        request(side).wait()
    req_copy = pltpu.make_async_copy(req_v, req_s, local_sem.at[3])
    req_copy.start()
    req_copy.wait()
    for side in (0, 1):
        for c in range(cap):
            stage[side, c] = p_loc[jnp.maximum(req_s[side, 1 - side, c], 0)]
        reply(side).start()

    index_copies[0].wait()

    def count(i, counts):
        return tuple(n + (agg_ref[i] == q).astype(jnp.int32) for q, n in enumerate(counts))

    counts = lax.fori_loop(0, shard_rows, count, (jnp.int32(0),) * grp_count)
    starts = [jnp.int32(0)]
    for n in counts:
        starts.append(starts[-1] + (n + 3) // 4)
    for q in range(grp_count):
        last_s[q] = jnp.where(counts[q] > 0, starts[q + 1], 0)
    for j in range(chunk_count):
        begins = jnp.int32(0)
        for q in range(grp_count):
            begins = jnp.where((starts[q] == j) & (counts[q] > 0), 1, begins)
        keep_s[j] = 1 - begins
    lanes = lax.broadcasted_iota(jnp.int32, order_v.shape, 1)

    def place(i, carry):
        heads, order = carry
        spot = jnp.int32(0)
        for q, head in enumerate(heads):
            spot = jnp.where(agg_ref[i] == q, head, spot)
        heads = tuple(head + (agg_ref[i] == q).astype(jnp.int32) for q, head in enumerate(heads))
        return heads, jnp.where(lanes == spot, i, order)

    heads = tuple(start * 4 for start in starts[:-1])
    _, order = lax.fori_loop(
        0, shard_rows, place, (heads, jnp.full(order_v.shape, shard_rows, jnp.int32))
    )
    order_v[...] = order
    order_copy = pltpu.make_async_copy(order_v, order_s, local_sem.at[7])
    order_copy.start()
    for copy in index_copies[1:]:
        copy.wait()
    order_copy.wait()

    @pl.loop(0, chunk_count, unroll=2)
    def _(j):
        blocks = [p_loc[order_s[0, 4 * j + n]] for n in range(4)]
        left[j] = jnp.concatenate(blocks, axis=0).T

    for part in (0, 1):
        sums[part, 0] = jnp.zeros(sums.shape[2:], jnp.float32)

    a_copy.wait()
    all_copy.wait()
    for side in (0, 1):
        reply(side).wait()

    def slot_sums(i, slots):
        columns = jnp.concatenate(
            [p_all[jnp.maximum(cols_ref[k, i], 0)] for k in range(slot_count)], axis=0
        )
        places = [
            jnp.where(cols_ref[k, i] >= 0, rap_ref[k, i], -1) for k in range(slot_count)
        ]
        spread = []
        for k in range(0, slot_count, 2):
            block = a_v[i, :, k * cells : (k + 2) * cells]
            place = lane_pair(places[k], places[k + 1], 16)
            keeps = [indicator(place, s) for s in slots]
            spread.append(
                jnp.concatenate(
                    [block * jnp.concatenate([keep] * (cells // 16), axis=0) for keep in keeps],
                    axis=0,
                )
            )
        product = jnp.dot(
            jnp.concatenate(spread, axis=1), columns, preferred_element_type=jnp.float32
        ).astype(jnp.bfloat16)
        for n, s in enumerate(slots):
            near[s // 4, i, :, s % 4 * 128 : (s % 4 + 1) * 128] = product[
                n * cells : (n + 1) * cells
            ]

    def chunk_sums(part):
        @pl.loop(0, chunk_count, unroll=2)
        def _(j):
            rows = [jnp.minimum(order_s[0, 4 * j + n], shard_rows - 1) for n in range(4)]
            right = jnp.concatenate([near[part, row] for row in rows], axis=0)
            keep = keep_s[j].astype(jnp.float32)
            sums[part, j + 1] = sums[part, j] * keep + jnp.dot(
                left[j], right, preferred_element_type=jnp.float32
            )

    first_half, second_half = range(CSLOT // 2), range(CSLOT // 2, CSLOT)

    @pl.loop(0, shard_rows, unroll=4)
    def _(i):
        slot_sums(i, first_half)

    chunk_sums(0)

    def hop(way, step, part, pair):
        return pltpu.make_async_remote_copy(
            src_ref=outgoing.at[way, step, part, pair],
            dst_ref=incoming.at[way, step, part, pair],
            send_sem=ring_send.at[way, step, part, pair],
            recv_sem=ring_recv.at[way, step, part, pair],
            device_id={"grp": (ahead, behind)[way]},
            device_id_type=MESH,
        )

    def term(part, q, slot):
        return sums[part, last_s[q], :, slot * 128 : (slot + 1) * 128]

    def advance(part, step):
        forth, back = half - step, grp_count - (half - 1 - step)
        if part == 1:
            forth, back = grp_count - forth, grp_count - back
        for pair in (0, 1):
            for away, way in ((forth, part), (back, 1 - part)):
                if way != part and step == half - 1:
                    continue
                q = lax.rem(grp + away, grp_count)
                if step > 0:
                    hop(way, step - 1, part, pair).wait_recv()
                for h in (0, 1):
                    total = term(part, q, pair * 2 + h)
                    if step > 0:
                        total = total + incoming[way, step - 1, part, pair, h].astype(jnp.float32)
                    outgoing[way, step, part, pair, h] = total.astype(jnp.bfloat16)
                hop(way, step, part, pair).start()

    def later_sums(first, end):
        @pl.loop(first, end, unroll=4)
        def _(i):
            slot_sums(i, second_half)

    advance(0, 0)
    later_sums(0, shard_rows // 2)
    if half > 2:
        advance(0, 1)
    later_sums(shard_rows // 2, shard_rows)
    chunk_sums(1)
    advance(1, 0)
    for step in range(2 if half > 2 else 1, half):
        advance(0, step)
        advance(1, step - 1)
    advance(1, half - 1)

    for way in (0, 1):
        for step in range(half - 1):
            for part in (0, 1):
                for pair in (0, 1):
                    hop(way, step, part, pair).wait_send()

    for part in (0, 1):
        for pair in (0, 1):
            hop(part, half - 1, part, pair).wait_recv()
            hop(1 - part, half - 2, part, pair).wait_recv()
            for h in (0, 1):
                slot = pair * 2 + h
                total_v[pl.ds((part * 4 + slot) * 128, 128)] = (
                    term(part, grp, slot)
                    + incoming[part, half - 1, part, pair, h].astype(jnp.float32)
                    + incoming[1 - part, half - 2, part, pair, h].astype(jnp.float32)
                )

    for d in range(128):
        out_ref[0, :, d * 128 : (d + 1) * 128] = total_v[pl.ds(d, CSLOT, stride=128)]

    for part in (0, 1):
        for pair in (0, 1):
            hop(part, half - 1, part, pair).wait_send()


def on_device(row_count, grp_count, a_blocks, prolong, a_cols, read_slots, agg, rap_slot):
    shard_rows, cells, width = a_blocks.shape
    coarse = prolong.shape[2]
    cap = read_slots.shape[1]
    half = grp_count // 2
    chunk_count = (shard_rows + 3 * grp_count) // 4
    vmem = pl.BlockSpec(memory_space=pltpu.VMEM)
    hbm = pl.BlockSpec(memory_space=pltpu.HBM)
    b16 = jnp.bfloat16
    dma = pltpu.SemaphoreType.DMA
    return pl.pallas_call(
        functools.partial(kernel, row_count, grp_count),
        out_shape=jax.ShapeDtypeStruct((1, CSLOT, coarse * coarse), jnp.float32),
        in_specs=[hbm] * 6,
        out_specs=vmem,
        scratch_shapes=[
            pltpu.SMEM(a_cols.shape[::-1], jnp.int32),
            pltpu.SMEM(agg.shape, jnp.int32),
            pltpu.SMEM(rap_slot.shape[::-1], jnp.int32),
            pltpu.VMEM((shard_rows, cells, width), b16),
            pltpu.VMEM((shard_rows + 1, cells, coarse), b16),
            pltpu.VMEM((shard_rows + 2 * cap, cells, coarse), b16),
            pltpu.VMEM((chunk_count, coarse, 4 * cells), b16),
            pltpu.VMEM((2, shard_rows, cells, CSLOT // 2 * coarse), b16),
            pltpu.VMEM((2, chunk_count + 1, coarse, CSLOT // 2 * coarse), jnp.float32),
            pltpu.VMEM((8, 128), jnp.int32),
            pltpu.SMEM((8, 128), jnp.int32),
            pltpu.SMEM((chunk_count,), jnp.int32),
            pltpu.SMEM((grp_count,), jnp.int32),
            pltpu.VMEM((CSLOT * coarse, coarse), jnp.float32),
            pltpu.VMEM((2, 2, cap), jnp.int32),
            pltpu.SMEM((2, 2, cap), jnp.int32),
            pltpu.VMEM((2, cap, cells, coarse), b16),
            pltpu.VMEM((2, half, 2, 2, 2, coarse, coarse), b16),
            pltpu.VMEM((2, half, 2, 2, 2, coarse, coarse), b16),
            dma((8,)),
            dma((2,)),
            dma((2,)),
            dma((2,)),
            dma((2,)),
            dma((2, half, 2, 2)),
            dma((2, half, 2, 2)),
        ],
        compiler_params=pltpu.CompilerParams(
            collective_id=0, has_side_effects=True, vmem_limit_bytes=56 * 1024 * 1024
        ),
    )(read_slots, a_cols.T, agg, rap_slot.T, a_blocks, prolong)

def solution(mesh):
    return jax.shard_map(
        functools.partial(on_device, mesh.shape["rows"], mesh.shape["grp"]),
        mesh=mesh,
        in_specs=(
            P(("rows", "grp"), None, None),
            P(("rows", "grp"), None, None),
            P(("rows", "grp"), None),
            P(("rows", "grp"), None),
            P(("rows", "grp")),
            P(("rows", "grp"), None),
        ),
        out_specs=P(("rows", "grp"), None, None),
        check_vma=False,
    )
```

```python
import functools

import jax
import jax.numpy as jnp
from jax import lax
from jax.experimental import pallas as pl
from jax.experimental.pallas import tpu as pltpu
from jax.sharding import PartitionSpec as P

CSLOT = 8
MESH = pl.DeviceIdType.MESH


def lane_pair(left, right, rows):
    lanes = lax.broadcasted_iota(jnp.int32, (rows, 128), 1)
    return jnp.where(lanes < 64, left, right)


def indicator(value, wanted):
    return jnp.where(value == wanted, 1.0, 0.0).astype(jnp.bfloat16)


def kernel(
    row_count, grp_count,
    reads_hbm, cols_hbm, agg_hbm, rap_hbm, a_hbm, p_hbm,
    out_ref,
    cols_ref, agg_ref, rap_ref,
    a_v, p_loc, p_all, left, near, sums, order_v, order_s, keep_s, last_s, total_v, req_v, req_s, stage, outgoing, incoming,
    local_sem, req_send, req_recv, rep_send, rep_recv, ring_send, ring_recv,
):
    shard_rows, cells, _ = a_v.shape
    slot_count = cols_ref.shape[0]
    cap = stage.shape[1]
    half = grp_count // 2
    chunk_count = left.shape[0]
    row, grp = lax.axis_index("rows"), lax.axis_index("grp")
    above, below = lax.rem(row + 1, row_count), lax.rem(row + row_count - 1, row_count)
    turn = 1 - 2 * lax.rem(row, 2)
    ahead, behind = (lax.rem(grp + sign * turn + grp_count, grp_count) for sign in (1, -1))

    a_copy = pltpu.make_async_copy(a_hbm, a_v, local_sem.at[0])
    p_copy = pltpu.make_async_copy(p_hbm, p_loc.at[pl.ds(0, shard_rows)], local_sem.at[1])
    all_copy = pltpu.make_async_copy(p_hbm, p_all.at[pl.ds(0, shard_rows)], local_sem.at[2])
    p_copy.start()
    a_copy.start()
    all_copy.start()
    index_copies = [
        pltpu.make_async_copy(source, target, local_sem.at[4 + n])
        for n, (source, target) in enumerate(
            ((agg_hbm, agg_ref), (cols_hbm, cols_ref), (rap_hbm, rap_ref))
        )
    ]
    for copy in index_copies:
        copy.start()

    barrier = pltpu.get_barrier_semaphore()
    for device in ({"rows": above}, {"rows": below}, {"grp": ahead}, {"grp": behind}):
        pl.semaphore_signal(barrier, inc=1, device_id=device, device_id_type=MESH)
    pl.semaphore_wait(barrier, 4)

    def request(side):
        return pltpu.make_async_remote_copy(
            src_ref=reads_hbm,
            dst_ref=req_v.at[1 - side],
            send_sem=req_send.at[side],
            recv_sem=req_recv.at[1 - side],
            device_id={"rows": (below, above)[side]},
            device_id_type=MESH,
        )

    def reply(side):
        return pltpu.make_async_remote_copy(
            src_ref=stage.at[side],
            dst_ref=p_all.at[pl.ds(shard_rows + (1 - side) * cap, cap)],
            send_sem=rep_send.at[side],
            recv_sem=rep_recv.at[1 - side],
            device_id={"rows": (below, above)[side]},
            device_id_type=MESH,
        )

    for side in (0, 1):
        request(side).start()

    p_copy.wait()
    p_loc[shard_rows] = jnp.zeros(p_loc.shape[1:], p_loc.dtype)
    for side in (0, 1):
        request(side).wait()
    req_copy = pltpu.make_async_copy(req_v, req_s, local_sem.at[3])
    req_copy.start()
    req_copy.wait()
    for side in (0, 1):
        for c in range(cap):
            stage[side, c] = p_loc[jnp.maximum(req_s[side, 1 - side, c], 0)]
        reply(side).start()

    index_copies[0].wait()

    def count(i, counts):
        return tuple(n + (agg_ref[i] == q).astype(jnp.int32) for q, n in enumerate(counts))

    counts = lax.fori_loop(0, shard_rows, count, (jnp.int32(0),) * grp_count)
    starts = [jnp.int32(0)]
    for n in counts:
        starts.append(starts[-1] + (n + 3) // 4)
    for q in range(grp_count):
        last_s[q] = jnp.where(counts[q] > 0, starts[q + 1], 0)
    for j in range(chunk_count):
        begins = jnp.int32(0)
        for q in range(grp_count):
            begins = jnp.where((starts[q] == j) & (counts[q] > 0), 1, begins)
        keep_s[j] = 1 - begins
    lanes = lax.broadcasted_iota(jnp.int32, order_v.shape, 1)

    def place(i, carry):
        heads, order = carry
        spot = jnp.int32(0)
        for q, head in enumerate(heads):
            spot = jnp.where(agg_ref[i] == q, head, spot)
        heads = tuple(head + (agg_ref[i] == q).astype(jnp.int32) for q, head in enumerate(heads))
        return heads, jnp.where(lanes == spot, i, order)

    heads = tuple(start * 4 for start in starts[:-1])
    _, order = lax.fori_loop(
        0, shard_rows, place, (heads, jnp.full(order_v.shape, shard_rows, jnp.int32))
    )
    order_v[...] = order
    order_copy = pltpu.make_async_copy(order_v, order_s, local_sem.at[7])
    order_copy.start()
    for copy in index_copies[1:]:
        copy.wait()
    order_copy.wait()

    @pl.loop(0, chunk_count, unroll=2)
    def _(j):
        blocks = [p_loc[order_s[0, 4 * j + n]] for n in range(4)]
        left[j] = jnp.concatenate(blocks, axis=0).T

    for part in (0, 1):
        sums[part, 0] = jnp.zeros(sums.shape[2:], jnp.float32)

    a_copy.wait()
    all_copy.wait()
    for side in (0, 1):
        reply(side).wait()

    def slot_sums(i, slots):
        columns = jnp.concatenate(
            [p_all[jnp.maximum(cols_ref[k, i], 0)] for k in range(slot_count)], axis=0
        )
        places = [
            jnp.where(cols_ref[k, i] >= 0, rap_ref[k, i], -1) for k in range(slot_count)
        ]
        spread = []
        for k in range(0, slot_count, 2):
            block = a_v[i, :, k * cells : (k + 2) * cells]
            place = lane_pair(places[k], places[k + 1], 16)
            keeps = [indicator(place, s) for s in slots]
            spread.append(
                jnp.concatenate(
                    [block * jnp.concatenate([keep] * (cells // 16), axis=0) for keep in keeps],
                    axis=0,
                )
            )
        product = jnp.dot(
            jnp.concatenate(spread, axis=1), columns, preferred_element_type=jnp.float32
        ).astype(jnp.bfloat16)
        for n, s in enumerate(slots):
            near[s // 4, i, :, s % 4 * 128 : (s % 4 + 1) * 128] = product[
                n * cells : (n + 1) * cells
            ]

    def chunk_sums(part):
        @pl.loop(0, chunk_count, unroll=2)
        def _(j):
            rows = [jnp.minimum(order_s[0, 4 * j + n], shard_rows - 1) for n in range(4)]
            right = jnp.concatenate([near[part, row] for row in rows], axis=0)
            keep = keep_s[j].astype(jnp.float32)
            sums[part, j + 1] = sums[part, j] * keep + jnp.dot(
                left[j], right, preferred_element_type=jnp.float32
            )

    first_half, second_half = range(CSLOT // 2), range(CSLOT // 2, CSLOT)

    @pl.loop(0, shard_rows, unroll=4)
    def _(i):
        slot_sums(i, first_half)

    chunk_sums(0)

    def hop(way, step, part, pair):
        return pltpu.make_async_remote_copy(
            src_ref=outgoing.at[way, step, part, pair],
            dst_ref=incoming.at[way, step, part, pair],
            send_sem=ring_send.at[way, step, part, pair],
            recv_sem=ring_recv.at[way, step, part, pair],
            device_id={"grp": (ahead, behind)[way]},
            device_id_type=MESH,
        )

    def term(part, q, slot):
        return sums[part, last_s[q], :, slot * 128 : (slot + 1) * 128]

    def advance(part, step):
        sign = 1 - 2 * part
        forth, back = sign * (half - step), -sign * (half - 1 - step)
        for pair in (0, 1):
            for away, way in ((forth, part), (back, 1 - part)):
                if way != part and step == half - 1:
                    continue
                q = lax.rem(grp + turn * away + grp_count, grp_count)
                if step > 0:
                    hop(way, step - 1, part, pair).wait_recv()
                for h in (0, 1):
                    total = term(part, q, pair * 2 + h)
                    if step > 0:
                        total = total + incoming[way, step - 1, part, pair, h].astype(jnp.float32)
                    outgoing[way, step, part, pair, h] = total.astype(jnp.bfloat16)
                hop(way, step, part, pair).start()

    def later_sums(first, end):
        @pl.loop(first, end, unroll=4)
        def _(i):
            slot_sums(i, second_half)

    advance(0, 0)
    later_sums(0, shard_rows // 2)
    if half > 2:
        advance(0, 1)
    later_sums(shard_rows // 2, shard_rows)
    chunk_sums(1)
    advance(1, 0)
    for step in range(2 if half > 2 else 1, half):
        advance(0, step)
        advance(1, step - 1)
    advance(1, half - 1)

    for way in (0, 1):
        for step in range(half - 1):
            for part in (0, 1):
                for pair in (0, 1):
                    hop(way, step, part, pair).wait_send()

    for part in (0, 1):
        for pair in (0, 1):
            hop(part, half - 1, part, pair).wait_recv()
            hop(1 - part, half - 2, part, pair).wait_recv()
            for h in (0, 1):
                slot = pair * 2 + h
                total_v[pl.ds((part * 4 + slot) * 128, 128)] = (
                    term(part, grp, slot)
                    + incoming[part, half - 1, part, pair, h].astype(jnp.float32)
                    + incoming[1 - part, half - 2, part, pair, h].astype(jnp.float32)
                )

    for d in range(128):
        out_ref[0, :, d * 128 : (d + 1) * 128] = total_v[pl.ds(d, CSLOT, stride=128)]

    for part in (0, 1):
        for pair in (0, 1):
            hop(part, half - 1, part, pair).wait_send()


def on_device(row_count, grp_count, a_blocks, prolong, a_cols, read_slots, agg, rap_slot):
    shard_rows, cells, width = a_blocks.shape
    coarse = prolong.shape[2]
    cap = read_slots.shape[1]
    half = grp_count // 2
    chunk_count = (shard_rows + 3 * grp_count) // 4
    vmem = pl.BlockSpec(memory_space=pltpu.VMEM)
    hbm = pl.BlockSpec(memory_space=pltpu.HBM)
    b16 = jnp.bfloat16
    dma = pltpu.SemaphoreType.DMA
    return pl.pallas_call(
        functools.partial(kernel, row_count, grp_count),
        out_shape=jax.ShapeDtypeStruct((1, CSLOT, coarse * coarse), jnp.float32),
        in_specs=[hbm] * 6,
        out_specs=vmem,
        scratch_shapes=[
            pltpu.SMEM(a_cols.shape[::-1], jnp.int32),
            pltpu.SMEM(agg.shape, jnp.int32),
            pltpu.SMEM(rap_slot.shape[::-1], jnp.int32),
            pltpu.VMEM((shard_rows, cells, width), b16),
            pltpu.VMEM((shard_rows + 1, cells, coarse), b16),
            pltpu.VMEM((shard_rows + 2 * cap, cells, coarse), b16),
            pltpu.VMEM((chunk_count, coarse, 4 * cells), b16),
            pltpu.VMEM((2, shard_rows, cells, CSLOT // 2 * coarse), b16),
            pltpu.VMEM((2, chunk_count + 1, coarse, CSLOT // 2 * coarse), jnp.float32),
            pltpu.VMEM((8, 128), jnp.int32),
            pltpu.SMEM((8, 128), jnp.int32),
            pltpu.SMEM((chunk_count,), jnp.int32),
            pltpu.SMEM((grp_count,), jnp.int32),
            pltpu.VMEM((CSLOT * coarse, coarse), jnp.float32),
            pltpu.VMEM((2, 2, cap), jnp.int32),
            pltpu.SMEM((2, 2, cap), jnp.int32),
            pltpu.VMEM((2, cap, cells, coarse), b16),
            pltpu.VMEM((2, half, 2, 2, 2, coarse, coarse), b16),
            pltpu.VMEM((2, half, 2, 2, 2, coarse, coarse), b16),
            dma((8,)),
            dma((2,)),
            dma((2,)),
            dma((2,)),
            dma((2,)),
            dma((2, half, 2, 2)),
            dma((2, half, 2, 2)),
        ],
        compiler_params=pltpu.CompilerParams(
            collective_id=0, has_side_effects=True, vmem_limit_bytes=56 * 1024 * 1024
        ),
    )(read_slots, a_cols.T, agg, rap_slot.T, a_blocks, prolong)

def solution(mesh):
    return jax.shard_map(
        functools.partial(on_device, mesh.shape["rows"], mesh.shape["grp"]),
        mesh=mesh,
        in_specs=(
            P(("rows", "grp"), None, None),
            P(("rows", "grp"), None, None),
            P(("rows", "grp"), None),
            P(("rows", "grp"), None),
            P(("rows", "grp")),
            P(("rows", "grp"), None),
        ),
        out_specs=P(("rows", "grp"), None, None),
        check_vma=False,
    )
```

```python
import functools

import jax
import jax.numpy as jnp
from jax import lax
from jax.experimental import pallas as pl
from jax.experimental.pallas import tpu as pltpu
from jax.sharding import PartitionSpec as P

CSLOT = 8
MESH = pl.DeviceIdType.MESH


def lane_pair(left, right, rows):
    lanes = lax.broadcasted_iota(jnp.int32, (rows, 128), 1)
    return jnp.where(lanes < 64, left, right)


def indicator(value, wanted):
    return jnp.where(value == wanted, 1.0, 0.0).astype(jnp.bfloat16)


def kernel(
    row_count, grp_count,
    reads_hbm, cols_hbm, agg_hbm, rap_hbm, a_hbm, p_hbm,
    out_ref,
    cols_ref, agg_ref, rap_ref,
    a_v, p_loc, p_all, p_turned, p_masked, near, total_v, req_v, req_s, stage, outgoing, incoming,
    local_sem, req_send, req_recv, rep_send, rep_recv, ring_send, ring_recv,
):
    shard_rows, cells, _ = a_v.shape
    slot_count = cols_ref.shape[0]
    cap = stage.shape[1]
    half = grp_count // 2
    row, grp = lax.axis_index("rows"), lax.axis_index("grp")
    above, below = lax.rem(row + 1, row_count), lax.rem(row + row_count - 1, row_count)
    ahead, behind = lax.rem(grp + 1, grp_count), lax.rem(grp + grp_count - 1, grp_count)

    a_copy = pltpu.make_async_copy(a_hbm, a_v, local_sem.at[0])
    p_copy = pltpu.make_async_copy(p_hbm, p_loc, local_sem.at[1])
    all_copy = pltpu.make_async_copy(p_hbm, p_all.at[pl.ds(0, shard_rows)], local_sem.at[2])
    p_copy.start()
    a_copy.start()
    all_copy.start()
    index_copies = [
        pltpu.make_async_copy(source, target, local_sem.at[4 + n])
        for n, (source, target) in enumerate(
            ((agg_hbm, agg_ref), (cols_hbm, cols_ref), (rap_hbm, rap_ref))
        )
    ]
    for copy in index_copies:
        copy.start()

    barrier = pltpu.get_barrier_semaphore()
    for device in ({"rows": above}, {"rows": below}, {"grp": ahead}, {"grp": behind}):
        pl.semaphore_signal(barrier, inc=1, device_id=device, device_id_type=MESH)
    pl.semaphore_wait(barrier, 4)

    def request(side):
        return pltpu.make_async_remote_copy(
            src_ref=reads_hbm,
            dst_ref=req_v.at[1 - side],
            send_sem=req_send.at[side],
            recv_sem=req_recv.at[1 - side],
            device_id={"rows": (below, above)[side]},
            device_id_type=MESH,
        )

    def reply(side):
        return pltpu.make_async_remote_copy(
            src_ref=stage.at[side],
            dst_ref=p_all.at[pl.ds(shard_rows + (1 - side) * cap, cap)],
            send_sem=rep_send.at[side],
            recv_sem=rep_recv.at[1 - side],
            device_id={"rows": (below, above)[side]},
            device_id_type=MESH,
        )

    for side in (0, 1):
        request(side).start()

    p_copy.wait()

    @pl.loop(0, shard_rows // 2, unroll=4)
    def _(pair):
        lanes = pl.ds(pl.multiple_of(pair * 128, 128), 128)
        p_turned[:, lanes] = p_loc[pl.ds(pair * 2, 2)].reshape(128, 128).T

    for side in (0, 1):
        request(side).wait()
    req_copy = pltpu.make_async_copy(req_v, req_s, local_sem.at[3])
    req_copy.start()
    req_copy.wait()
    for side in (0, 1):
        for c in range(cap):
            stage[side, c] = p_loc[jnp.maximum(req_s[side, 1 - side, c], 0)]
        reply(side).start()

    for copy in index_copies:
        copy.wait()

    @pl.loop(0, shard_rows // 2)
    def _(pair):
        lanes = pl.ds(pl.multiple_of(pair * 128, 128), 128)
        block = p_turned[:, lanes]
        owner = lane_pair(agg_ref[pair * 2], agg_ref[pair * 2 + 1], 16)
        for q in range(grp_count):
            keep = indicator(owner, q)
            p_masked[q, :, lanes] = block * jnp.concatenate([keep] * 8, axis=0)

    a_copy.wait()
    all_copy.wait()
    for side in (0, 1):
        reply(side).wait()

    def slot_sums(i, slots):
        columns = jnp.concatenate(
            [p_all[jnp.maximum(cols_ref[k, i], 0)] for k in range(slot_count)], axis=0
        )
        places = [
            jnp.where(cols_ref[k, i] >= 0, rap_ref[k, i], -1) for k in range(slot_count)
        ]
        spread = []
        for k in range(0, slot_count, 2):
            block = a_v[i, :, k * cells : (k + 2) * cells]
            place = lane_pair(places[k], places[k + 1], 16)
            keeps = [indicator(place, s) for s in slots]
            spread.append(
                jnp.concatenate(
                    [block * jnp.concatenate([keep] * (cells // 16), axis=0) for keep in keeps],
                    axis=0,
                )
            )
        product = jnp.dot(
            jnp.concatenate(spread, axis=1), columns, preferred_element_type=jnp.float32
        ).astype(jnp.bfloat16)
        rows = pl.ds(pl.multiple_of(i * cells, cells), cells)
        for n, s in enumerate(slots):
            near[s // 2, rows, (s % 2) * 128 : (s % 2 + 1) * 128] = product[
                n * cells : (n + 1) * cells
            ]

    def quarter(pair):
        @pl.loop(0, shard_rows, unroll=min(8, shard_rows))
        def _(i):
            slot_sums(i, (2 * pair, 2 * pair + 1))

    def hop(way, step, part, pair):
        return pltpu.make_async_remote_copy(
            src_ref=outgoing.at[way, step, part, pair],
            dst_ref=incoming.at[way, step, part, pair],
            send_sem=ring_send.at[way, step, part, pair],
            recv_sem=ring_recv.at[way, step, part, pair],
            device_id={"grp": (ahead, behind)[way]},
            device_id_type=MESH,
        )

    def advance(part, step, pair):
        forth, back = half - step, grp_count - (half - 1 - step)
        if part == 1:
            forth, back = grp_count - forth, grp_count - back
        far, near_by = lax.rem(grp + forth, grp_count), lax.rem(grp + back, grp_count)
        left = jnp.concatenate([p_masked[far], p_masked[near_by]], axis=0)
        terms = jnp.dot(left, near[part * 2 + pair], preferred_element_type=jnp.float32)
        for side, way in ((0, part), (1, 1 - part)):
            last = side == 1 and step == half - 1
            if step > 0 and not last:
                hop(way, step - 1, part, pair).wait_recv()
            for h in (0, 1):
                total = terms[side * 128 : (side + 1) * 128, h * 128 : (h + 1) * 128]
                if last:
                    slot = part * 4 + pair * 2 + h
                    total_v[pl.ds(pl.multiple_of(slot * 128, 128), 128)] = total
                    continue
                if step > 0:
                    total = total + incoming[way, step - 1, part, pair, h].astype(jnp.float32)
                outgoing[way, step, part, pair, h] = total.astype(jnp.bfloat16)
            if not last:
                hop(way, step, part, pair).start()

    def advance_both(part, step):
        @pl.loop(0, 2)
        def _(pair):
            advance(part, step, pair)

    quarter(0)
    advance(0, 0, 0)
    quarter(1)
    advance(0, 0, 1)
    advance(0, 1, 0)
    quarter(2)
    advance(0, 1, 1)
    quarter(3)
    advance_both(1, 0)
    for step in range(2, half):
        advance_both(0, step)
        advance_both(1, step - 1)
    advance_both(1, half - 1)

    for way in (0, 1):
        for step in range(half - 1):
            for part in (0, 1):
                for pair in (0, 1):
                    hop(way, step, part, pair).wait_send()

    for part in (0, 1):
        for pair in (0, 1):
            hop(part, half - 1, part, pair).wait_recv()
            hop(1 - part, half - 2, part, pair).wait_recv()
            for h in (0, 1):
                rows = pl.ds((part * 4 + pair * 2 + h) * 128, 128)
                total_v[rows] = (
                    total_v[rows]
                    + incoming[part, half - 1, part, pair, h].astype(jnp.float32)
                    + incoming[1 - part, half - 2, part, pair, h].astype(jnp.float32)
                )

    for d in range(128):
        out_ref[0, :, d * 128 : (d + 1) * 128] = total_v[pl.ds(d, CSLOT, stride=128)]

    for part in (0, 1):
        for pair in (0, 1):
            hop(part, half - 1, part, pair).wait_send()


def on_device(row_count, grp_count, a_blocks, prolong, a_cols, read_slots, agg, rap_slot):
    shard_rows, cells, width = a_blocks.shape
    coarse = prolong.shape[2]
    cap = read_slots.shape[1]
    half = grp_count // 2
    vmem = pl.BlockSpec(memory_space=pltpu.VMEM)
    hbm = pl.BlockSpec(memory_space=pltpu.HBM)
    b16 = jnp.bfloat16
    dma = pltpu.SemaphoreType.DMA
    return pl.pallas_call(
        functools.partial(kernel, row_count, grp_count),
        out_shape=jax.ShapeDtypeStruct((1, CSLOT, coarse * coarse), jnp.float32),
        in_specs=[hbm] * 6,
        out_specs=vmem,
        scratch_shapes=[
            pltpu.SMEM(a_cols.shape[::-1], jnp.int32),
            pltpu.SMEM(agg.shape, jnp.int32),
            pltpu.SMEM(rap_slot.shape[::-1], jnp.int32),
            pltpu.VMEM((shard_rows, cells, width), b16),
            pltpu.VMEM((shard_rows, cells, coarse), b16),
            pltpu.VMEM((shard_rows + 2 * cap, cells, coarse), b16),
            pltpu.VMEM((coarse, shard_rows * cells), b16),
            pltpu.VMEM((grp_count, coarse, shard_rows * cells), b16),
            pltpu.VMEM((CSLOT // 2, shard_rows * cells, 2 * coarse), b16),
            pltpu.VMEM((CSLOT * coarse, coarse), jnp.float32),
            pltpu.VMEM((2, 2, cap), jnp.int32),
            pltpu.SMEM((2, 2, cap), jnp.int32),
            pltpu.VMEM((2, cap, cells, coarse), b16),
            pltpu.VMEM((2, half, 2, 2, 2, coarse, coarse), b16),
            pltpu.VMEM((2, half, 2, 2, 2, coarse, coarse), b16),
            dma((7,)),
            dma((2,)),
            dma((2,)),
            dma((2,)),
            dma((2,)),
            dma((2, half, 2, 2)),
            dma((2, half, 2, 2)),
        ],
        compiler_params=pltpu.CompilerParams(
            collective_id=0, has_side_effects=True, vmem_limit_bytes=56 * 1024 * 1024
        ),
    )(read_slots, a_cols.T, agg, rap_slot.T, a_blocks, prolong)

def solution(mesh):
    return jax.shard_map(
        functools.partial(on_device, mesh.shape["rows"], mesh.shape["grp"]),
        mesh=mesh,
        in_specs=(
            P(("rows", "grp"), None, None),
            P(("rows", "grp"), None, None),
            P(("rows", "grp"), None),
            P(("rows", "grp"), None),
            P(("rows", "grp")),
            P(("rows", "grp"), None),
        ),
        out_specs=P(("rows", "grp"), None, None),
        check_vma=False,
    )
```

```python
import functools

import jax
import jax.numpy as jnp
from jax import lax
from jax.experimental import pallas as pl
from jax.experimental.pallas import tpu as pltpu
from jax.sharding import PartitionSpec as P

CSLOT = 8
MESH = pl.DeviceIdType.MESH


def lane_pair(left, right, rows):
    lanes = lax.broadcasted_iota(jnp.int32, (rows, 128), 1)
    return jnp.where(lanes < 64, left, right)


def indicator(value, wanted):
    return jnp.where(value == wanted, 1.0, 0.0).astype(jnp.bfloat16)


def kernel(
    row_count, grp_count,
    reads_hbm, cols_hbm, agg_hbm, rap_hbm, a_hbm, p_hbm,
    out_ref,
    cols_ref, agg_ref, rap_ref,
    a_v, p_loc, p_all, p_turned, p_masked, near, total_v, req_v, req_s, stage, outgoing, incoming,
    local_sem, req_send, req_recv, rep_send, rep_recv, ring_send, ring_recv,
):
    shard_rows, cells, _ = a_v.shape
    slot_count = cols_ref.shape[0]
    cap = stage.shape[1]
    half = grp_count // 2
    row, grp = lax.axis_index("rows"), lax.axis_index("grp")
    above, below = lax.rem(row + 1, row_count), lax.rem(row + row_count - 1, row_count)
    ahead, behind = lax.rem(grp + 1, grp_count), lax.rem(grp + grp_count - 1, grp_count)

    a_copy = pltpu.make_async_copy(a_hbm, a_v, local_sem.at[0])
    p_copy = pltpu.make_async_copy(p_hbm, p_loc, local_sem.at[1])
    all_copy = pltpu.make_async_copy(p_hbm, p_all.at[pl.ds(0, shard_rows)], local_sem.at[2])
    p_copy.start()
    a_copy.start()
    all_copy.start()
    index_copies = [
        pltpu.make_async_copy(source, target, local_sem.at[4 + n])
        for n, (source, target) in enumerate(
            ((agg_hbm, agg_ref), (cols_hbm, cols_ref), (rap_hbm, rap_ref))
        )
    ]
    for copy in index_copies:
        copy.start()

    barrier = pltpu.get_barrier_semaphore()
    for device in ({"rows": above}, {"rows": below}, {"grp": ahead}, {"grp": behind}):
        pl.semaphore_signal(barrier, inc=1, device_id=device, device_id_type=MESH)
    pl.semaphore_wait(barrier, 4)

    def request(side):
        return pltpu.make_async_remote_copy(
            src_ref=reads_hbm,
            dst_ref=req_v.at[1 - side],
            send_sem=req_send.at[side],
            recv_sem=req_recv.at[1 - side],
            device_id={"rows": (below, above)[side]},
            device_id_type=MESH,
        )

    def reply(side):
        return pltpu.make_async_remote_copy(
            src_ref=stage.at[side],
            dst_ref=p_all.at[pl.ds(shard_rows + (1 - side) * cap, cap)],
            send_sem=rep_send.at[side],
            recv_sem=rep_recv.at[1 - side],
            device_id={"rows": (below, above)[side]},
            device_id_type=MESH,
        )

    for side in (0, 1):
        request(side).start()

    p_copy.wait()

    for side in (0, 1):
        request(side).wait()
    req_copy = pltpu.make_async_copy(req_v, req_s, local_sem.at[3])
    req_copy.start()
    req_copy.wait()
    for side in (0, 1):
        for c in range(cap):
            stage[side, c] = p_loc[jnp.maximum(req_s[side, 1 - side, c], 0)]
        reply(side).start()

    for copy in index_copies:
        copy.wait()

    @pl.loop(0, shard_rows // 2, unroll=4)
    def _(pair):
        lanes = pl.ds(pl.multiple_of(pair * 128, 128), 128)
        p_turned[:, lanes] = p_loc[pl.ds(pair * 2, 2)].reshape(128, 128).T

    def mask_rows(offsets):
        wanted = [lax.rem(grp + offset, grp_count) for offset in offsets]

        @pl.loop(0, shard_rows // 2, unroll=2)
        def _(pair):
            lanes = pl.ds(pl.multiple_of(pair * 128, 128), 128)
            block = p_turned[:, lanes]
            owner = lane_pair(agg_ref[pair * 2], agg_ref[pair * 2 + 1], 16)
            for q in wanted:
                keep = indicator(owner, q)
                p_masked[q, :, lanes] = block * jnp.concatenate([keep] * 8, axis=0)

    first_wanted = (half, half + 1, half - 1)
    mask_rows(first_wanted)

    a_copy.wait()
    all_copy.wait()
    for side in (0, 1):
        reply(side).wait()

    def slot_sums(i, slots):
        columns = jnp.concatenate(
            [p_all[jnp.maximum(cols_ref[k, i], 0)] for k in range(slot_count)], axis=0
        )
        places = [
            jnp.where(cols_ref[k, i] >= 0, rap_ref[k, i], -1) for k in range(slot_count)
        ]
        spread = []
        for k in range(0, slot_count, 2):
            block = a_v[i, :, k * cells : (k + 2) * cells]
            place = lane_pair(places[k], places[k + 1], 16)
            keeps = [indicator(place, s) for s in slots]
            spread.append(
                jnp.concatenate(
                    [block * jnp.concatenate([keep] * (cells // 16), axis=0) for keep in keeps],
                    axis=0,
                )
            )
        product = jnp.dot(
            jnp.concatenate(spread, axis=1), columns, preferred_element_type=jnp.float32
        ).astype(jnp.bfloat16)
        rows = pl.ds(pl.multiple_of(i * cells, cells), cells)
        for n, s in enumerate(slots):
            near[s // 2, rows, (s % 2) * 128 : (s % 2 + 1) * 128] = product[
                n * cells : (n + 1) * cells
            ]

    def quarter(pair):
        @pl.loop(0, shard_rows, unroll=min(8, shard_rows))
        def _(i):
            slot_sums(i, (2 * pair, 2 * pair + 1))

    def hop(way, step, part, pair):
        return pltpu.make_async_remote_copy(
            src_ref=outgoing.at[way, step, part, pair],
            dst_ref=incoming.at[way, step, part, pair],
            send_sem=ring_send.at[way, step, part, pair],
            recv_sem=ring_recv.at[way, step, part, pair],
            device_id={"grp": lax.rem(grp + 1 + way * (grp_count - 2), grp_count)},
            device_id_type=MESH,
        )

    def advance(part, step, pair):
        turn = 1 - 2 * pair
        far = lax.rem(grp + grp_count + turn * (half - step), grp_count)
        near_by = lax.rem(grp + grp_count - turn * (half - 1 - step), grp_count)
        left = jnp.concatenate([p_masked[far], p_masked[near_by]], axis=0)
        terms = jnp.dot(left, near[part * 2 + pair], preferred_element_type=jnp.float32)
        for side, way in ((0, pair), (1, 1 - pair)):
            last = side == 1 and step == half - 1
            if step > 0 and not last:
                hop(way, step - 1, part, pair).wait_recv()
            for h in (0, 1):
                total = terms[side * 128 : (side + 1) * 128, h * 128 : (h + 1) * 128]
                if last:
                    slot = part * 4 + pair * 2 + h
                    total_v[pl.ds(pl.multiple_of(slot * 128, 128), 128)] = total
                    continue
                if step > 0:
                    total = total + incoming[way, step - 1, part, pair, h].astype(jnp.float32)
                outgoing[way, step, part, pair, h] = total.astype(jnp.bfloat16)
            if not last:
                hop(way, step, part, pair).start()

    def advance_both(part, step):
        @pl.loop(0, 2)
        def _(pair):
            advance(part, step, pair)

    quarter(0)
    advance(0, 0, 0)
    quarter(1)
    advance(0, 0, 1)
    mask_rows([offset for offset in range(grp_count) if offset not in first_wanted])
    advance(0, 1, 0)
    quarter(2)
    advance(0, 1, 1)
    quarter(3)
    advance_both(1, 0)
    for step in range(2, half):
        advance_both(0, step)
        advance_both(1, step - 1)
    advance_both(1, half - 1)

    for way in (0, 1):
        for step in range(half - 1):
            for part in (0, 1):
                for pair in (0, 1):
                    hop(way, step, part, pair).wait_send()

    for part in (0, 1):
        for pair in (0, 1):
            hop(pair, half - 1, part, pair).wait_recv()
            hop(1 - pair, half - 2, part, pair).wait_recv()
            for h in (0, 1):
                rows = pl.ds((part * 4 + pair * 2 + h) * 128, 128)
                total_v[rows] = (
                    total_v[rows]
                    + incoming[pair, half - 1, part, pair, h].astype(jnp.float32)
                    + incoming[1 - pair, half - 2, part, pair, h].astype(jnp.float32)
                )

    for d in range(128):
        out_ref[0, :, d * 128 : (d + 1) * 128] = total_v[pl.ds(d, CSLOT, stride=128)]

    for part in (0, 1):
        for pair in (0, 1):
            hop(pair, half - 1, part, pair).wait_send()


def on_device(row_count, grp_count, a_blocks, prolong, a_cols, read_slots, agg, rap_slot):
    shard_rows, cells, width = a_blocks.shape
    coarse = prolong.shape[2]
    cap = read_slots.shape[1]
    half = grp_count // 2
    vmem = pl.BlockSpec(memory_space=pltpu.VMEM)
    hbm = pl.BlockSpec(memory_space=pltpu.HBM)
    b16 = jnp.bfloat16
    dma = pltpu.SemaphoreType.DMA
    return pl.pallas_call(
        functools.partial(kernel, row_count, grp_count),
        out_shape=jax.ShapeDtypeStruct((1, CSLOT, coarse * coarse), jnp.float32),
        in_specs=[hbm] * 6,
        out_specs=vmem,
        scratch_shapes=[
            pltpu.SMEM(a_cols.shape[::-1], jnp.int32),
            pltpu.SMEM(agg.shape, jnp.int32),
            pltpu.SMEM(rap_slot.shape[::-1], jnp.int32),
            pltpu.VMEM((shard_rows, cells, width), b16),
            pltpu.VMEM((shard_rows, cells, coarse), b16),
            pltpu.VMEM((shard_rows + 2 * cap, cells, coarse), b16),
            pltpu.VMEM((coarse, shard_rows * cells), b16),
            pltpu.VMEM((grp_count, coarse, shard_rows * cells), b16),
            pltpu.VMEM((CSLOT // 2, shard_rows * cells, 2 * coarse), b16),
            pltpu.VMEM((CSLOT * coarse, coarse), jnp.float32),
            pltpu.VMEM((2, 2, cap), jnp.int32),
            pltpu.SMEM((2, 2, cap), jnp.int32),
            pltpu.VMEM((2, cap, cells, coarse), b16),
            pltpu.VMEM((2, half, 2, 2, 2, coarse, coarse), b16),
            pltpu.VMEM((2, half, 2, 2, 2, coarse, coarse), b16),
            dma((7,)),
            dma((2,)),
            dma((2,)),
            dma((2,)),
            dma((2,)),
            dma((2, half, 2, 2)),
            dma((2, half, 2, 2)),
        ],
        compiler_params=pltpu.CompilerParams(
            collective_id=0, has_side_effects=True, vmem_limit_bytes=56 * 1024 * 1024
        ),
    )(read_slots, a_cols.T, agg, rap_slot.T, a_blocks, prolong)

def solution(mesh):
    return jax.shard_map(
        functools.partial(on_device, mesh.shape["rows"], mesh.shape["grp"]),
        mesh=mesh,
        in_specs=(
            P(("rows", "grp"), None, None),
            P(("rows", "grp"), None, None),
            P(("rows", "grp"), None),
            P(("rows", "grp"), None),
            P(("rows", "grp")),
            P(("rows", "grp"), None),
        ),
        out_specs=P(("rows", "grp"), None, None),
        check_vma=False,
    )
```

```python
import functools

import jax
import jax.numpy as jnp
from jax import lax
from jax.experimental import pallas as pl
from jax.experimental.pallas import tpu as pltpu
from jax.sharding import PartitionSpec as P

CSLOT = 8
MESH = pl.DeviceIdType.MESH


def lane_pair(left, right, rows):
    lanes = lax.broadcasted_iota(jnp.int32, (rows, 128), 1)
    return jnp.where(lanes < 64, left, right)


def indicator(value, wanted):
    return jnp.where(value == wanted, 1.0, 0.0).astype(jnp.bfloat16)


def kernel(
    row_count, grp_count,
    reads_hbm, cols_hbm, agg_hbm, rap_hbm, a_hbm, p_hbm,
    out_ref,
    cols_ref, agg_ref, rap_ref,
    a_v, p_loc, p_all, p_turned, p_masked, near, total_v, req_v, req_s, stage, outgoing, incoming,
    local_sem, req_send, req_recv, rep_send, rep_recv, ring_send, ring_recv,
):
    shard_rows, cells, _ = a_v.shape
    slot_count = cols_ref.shape[0]
    cap = stage.shape[1]
    half = grp_count // 2
    row, grp = lax.axis_index("rows"), lax.axis_index("grp")
    above, below = lax.rem(row + 1, row_count), lax.rem(row + row_count - 1, row_count)
    ahead, behind = lax.rem(grp + 1, grp_count), lax.rem(grp + grp_count - 1, grp_count)

    a_copy = pltpu.make_async_copy(a_hbm, a_v, local_sem.at[0])
    p_copy = pltpu.make_async_copy(p_hbm, p_loc, local_sem.at[1])
    all_copy = pltpu.make_async_copy(p_hbm, p_all.at[pl.ds(0, shard_rows)], local_sem.at[2])
    p_copy.start()
    a_copy.start()
    all_copy.start()
    index_copies = [
        pltpu.make_async_copy(source, target, local_sem.at[4 + n])
        for n, (source, target) in enumerate(
            ((agg_hbm, agg_ref), (cols_hbm, cols_ref), (rap_hbm, rap_ref))
        )
    ]
    for copy in index_copies:
        copy.start()

    barrier = pltpu.get_barrier_semaphore()
    for device in ({"rows": above}, {"rows": below}, {"grp": ahead}, {"grp": behind}):
        pl.semaphore_signal(barrier, inc=1, device_id=device, device_id_type=MESH)
    pl.semaphore_wait(barrier, 4)

    def request(side):
        return pltpu.make_async_remote_copy(
            src_ref=reads_hbm,
            dst_ref=req_v.at[1 - side],
            send_sem=req_send.at[side],
            recv_sem=req_recv.at[1 - side],
            device_id={"rows": (below, above)[side]},
            device_id_type=MESH,
        )

    def reply(side):
        return pltpu.make_async_remote_copy(
            src_ref=stage.at[side],
            dst_ref=p_all.at[pl.ds(shard_rows + (1 - side) * cap, cap)],
            send_sem=rep_send.at[side],
            recv_sem=rep_recv.at[1 - side],
            device_id={"rows": (below, above)[side]},
            device_id_type=MESH,
        )

    for side in (0, 1):
        request(side).start()

    p_copy.wait()

    @pl.loop(0, shard_rows // 2, unroll=4)
    def _(pair):
        lanes = pl.ds(pl.multiple_of(pair * 128, 128), 128)
        p_turned[:, lanes] = p_loc[pl.ds(pair * 2, 2)].reshape(128, 128).T

    for side in (0, 1):
        request(side).wait()
    req_copy = pltpu.make_async_copy(req_v, req_s, local_sem.at[3])
    req_copy.start()
    req_copy.wait()
    for side in (0, 1):
        for c in range(cap):
            stage[side, c] = p_loc[jnp.maximum(req_s[side, 1 - side, c], 0)]
        reply(side).start()

    for copy in index_copies:
        copy.wait()

    @pl.loop(0, shard_rows // 2)
    def _(pair):
        lanes = pl.ds(pl.multiple_of(pair * 128, 128), 128)
        block = p_turned[:, lanes]
        owner = lane_pair(agg_ref[pair * 2], agg_ref[pair * 2 + 1], 16)
        for q in range(grp_count):
            keep = indicator(owner, q)
            p_masked[q, :, lanes] = block * jnp.concatenate([keep] * 8, axis=0)

    a_copy.wait()
    all_copy.wait()
    for side in (0, 1):
        reply(side).wait()

    def slot_sums(i, pair):
        columns = jnp.concatenate(
            [p_all[jnp.maximum(cols_ref[k, i], 0)] for k in range(slot_count)], axis=0
        )
        places = [
            jnp.where(cols_ref[k, i] >= 0, rap_ref[k, i], -1) for k in range(slot_count)
        ]
        spread = []
        for k in range(0, slot_count, 2):
            block = a_v[i, :, k * cells : (k + 2) * cells]
            place = lane_pair(places[k], places[k + 1], 16)
            keeps = [indicator(place, 2 * pair + h) for h in (0, 1)]
            spread.append(
                jnp.concatenate(
                    [block * jnp.concatenate([keep] * (cells // 16), axis=0) for keep in keeps],
                    axis=0,
                )
            )
        product = jnp.dot(
            jnp.concatenate(spread, axis=1), columns, preferred_element_type=jnp.float32
        ).astype(jnp.bfloat16)
        rows = pl.ds(pl.multiple_of(i * cells, cells), cells)
        for h in (0, 1):
            near[pair, rows, h * 128 : (h + 1) * 128] = product[h * cells : (h + 1) * cells]

    def quarter(pair):
        @pl.loop(0, shard_rows, unroll=min(8, shard_rows))
        def _(i):
            slot_sums(i, pair)

    def hop(way, step, pair):
        return pltpu.make_async_remote_copy(
            src_ref=outgoing.at[way, step, pair],
            dst_ref=incoming.at[way, step, pair],
            send_sem=ring_send.at[way, step, pair],
            recv_sem=ring_recv.at[way, step, pair],
            device_id={"grp": lax.rem(grp + 1 + way * (grp_count - 2), grp_count)},
            device_id_type=MESH,
        )

    def advance(pair, step, first=False, last=False):
        long = pair // 2
        turn = 1 - 2 * long
        far = lax.rem(grp + grp_count + turn * (half - step), grp_count)
        near_by = lax.rem(grp + grp_count - turn * (half - 1 - step), grp_count)
        left = jnp.concatenate([p_masked[far], p_masked[near_by]], axis=0)
        terms = jnp.dot(left, near[pair], preferred_element_type=jnp.float32)
        for side, way in ((0, long), (1, 1 - long)):
            own = last and side == 1
            if not first and not own:
                hop(way, step - 1, pair).wait_recv()
            for h in (0, 1):
                total = terms[side * 128 : (side + 1) * 128, h * 128 : (h + 1) * 128]
                if own:
                    total_v[pl.ds(pl.multiple_of((pair * 2 + h) * 128, 128), 128)] = total
                    continue
                if not first:
                    total = total + incoming[way, step - 1, pair, h].astype(jnp.float32)
                outgoing[way, step, pair, h] = total.astype(jnp.bfloat16)
            if not own:
                hop(way, step, pair).start()

    @pl.loop(0, 4)
    def _(pair):
        quarter(pair)
        advance(pair, 0, first=True)

        @pl.loop(1, jnp.minimum(pair, half - 2) + 1)
        def _(step):
            advance(pair - step, step)

    advance(0, half - 1, last=True)

    @pl.loop(1, 4)
    def _(pair):
        @pl.loop(pair, half - 1)
        def _(step):
            advance(3 - (step - pair), step)

        advance(pair, half - 1, last=True)

    @pl.loop(0, 4)
    def _(pair):
        long = pair // 2

        @pl.loop(0, half - 1)
        def _(step):
            hop(0, step, pair).wait_send()
            hop(1, step, pair).wait_send()

        hop(long, half - 1, pair).wait_recv()
        hop(1 - long, half - 2, pair).wait_recv()
        for h in (0, 1):
            rows = pl.ds(pl.multiple_of((pair * 2 + h) * 128, 128), 128)
            total_v[rows] = (
                total_v[rows]
                + incoming[long, half - 1, pair, h].astype(jnp.float32)
                + incoming[1 - long, half - 2, pair, h].astype(jnp.float32)
            )

    for d in range(128):
        out_ref[0, :, d * 128 : (d + 1) * 128] = total_v[pl.ds(d, CSLOT, stride=128)]

    for pair in range(4):
        hop(pair // 2, half - 1, pair).wait_send()


def on_device(row_count, grp_count, a_blocks, prolong, a_cols, read_slots, agg, rap_slot):
    shard_rows, cells, width = a_blocks.shape
    coarse = prolong.shape[2]
    cap = read_slots.shape[1]
    half = grp_count // 2
    vmem = pl.BlockSpec(memory_space=pltpu.VMEM)
    hbm = pl.BlockSpec(memory_space=pltpu.HBM)
    b16 = jnp.bfloat16
    dma = pltpu.SemaphoreType.DMA
    return pl.pallas_call(
        functools.partial(kernel, row_count, grp_count),
        out_shape=jax.ShapeDtypeStruct((1, CSLOT, coarse * coarse), jnp.float32),
        in_specs=[hbm] * 6,
        out_specs=vmem,
        scratch_shapes=[
            pltpu.SMEM(a_cols.shape[::-1], jnp.int32),
            pltpu.SMEM(agg.shape, jnp.int32),
            pltpu.SMEM(rap_slot.shape[::-1], jnp.int32),
            pltpu.VMEM((shard_rows, cells, width), b16),
            pltpu.VMEM((shard_rows, cells, coarse), b16),
            pltpu.VMEM((shard_rows + 2 * cap, cells, coarse), b16),
            pltpu.VMEM((coarse, shard_rows * cells), b16),
            pltpu.VMEM((grp_count, coarse, shard_rows * cells), b16),
            pltpu.VMEM((CSLOT // 2, shard_rows * cells, 2 * coarse), b16),
            pltpu.VMEM((CSLOT * coarse, coarse), jnp.float32),
            pltpu.VMEM((2, 2, cap), jnp.int32),
            pltpu.SMEM((2, 2, cap), jnp.int32),
            pltpu.VMEM((2, cap, cells, coarse), b16),
            pltpu.VMEM((2, half, 4, 2, coarse, coarse), b16),
            pltpu.VMEM((2, half, 4, 2, coarse, coarse), b16),
            dma((7,)),
            dma((2,)),
            dma((2,)),
            dma((2,)),
            dma((2,)),
            dma((2, half, 4)),
            dma((2, half, 4)),
        ],
        compiler_params=pltpu.CompilerParams(
            collective_id=0, has_side_effects=True, vmem_limit_bytes=56 * 1024 * 1024
        ),
    )(read_slots, a_cols.T, agg, rap_slot.T, a_blocks, prolong)

def solution(mesh):
    return jax.shard_map(
        functools.partial(on_device, mesh.shape["rows"], mesh.shape["grp"]),
        mesh=mesh,
        in_specs=(
            P(("rows", "grp"), None, None),
            P(("rows", "grp"), None, None),
            P(("rows", "grp"), None),
            P(("rows", "grp"), None),
            P(("rows", "grp")),
            P(("rows", "grp"), None),
        ),
        out_specs=P(("rows", "grp"), None, None),
        check_vma=False,
    )
```

```python
import functools

import jax
import jax.numpy as jnp
from jax import lax
from jax.experimental import pallas as pl
from jax.experimental.pallas import tpu as pltpu
from jax.sharding import PartitionSpec as P

CSLOT = 8
MESH = pl.DeviceIdType.MESH


def lane_pair(left, right, rows):
    lanes = lax.broadcasted_iota(jnp.int32, (rows, 128), 1)
    return jnp.where(lanes < 64, left, right)


def indicator(value, wanted):
    return jnp.where(value == wanted, 1.0, 0.0).astype(jnp.bfloat16)


def kernel(
    row_count, grp_count,
    reads_hbm, cols_hbm, agg_hbm, rap_hbm, a_hbm, p_hbm,
    out_ref,
    cols_ref, agg_ref, rap_ref,
    a_v, p_loc, p_all, p_turned, p_masked, near, total_v, req_v, req_s, stage, outgoing, incoming,
    local_sem, req_send, req_recv, rep_send, rep_recv, ring_send, ring_recv,
):
    shard_rows, cells, _ = a_v.shape
    slot_count = cols_ref.shape[0]
    cap = stage.shape[1]
    half = grp_count // 2
    row, grp = lax.axis_index("rows"), lax.axis_index("grp")
    above, below = lax.rem(row + 1, row_count), lax.rem(row + row_count - 1, row_count)
    ahead, behind = lax.rem(grp + 1, grp_count), lax.rem(grp + grp_count - 1, grp_count)

    a_copy = pltpu.make_async_copy(a_hbm, a_v, local_sem.at[0])
    p_copy = pltpu.make_async_copy(p_hbm, p_loc, local_sem.at[1])
    all_copy = pltpu.make_async_copy(p_hbm, p_all.at[pl.ds(0, shard_rows)], local_sem.at[2])
    p_copy.start()
    a_copy.start()
    all_copy.start()
    index_copies = [
        pltpu.make_async_copy(source, target, local_sem.at[4 + n])
        for n, (source, target) in enumerate(
            ((agg_hbm, agg_ref), (cols_hbm, cols_ref), (rap_hbm, rap_ref))
        )
    ]
    for copy in index_copies:
        copy.start()

    barrier = pltpu.get_barrier_semaphore()
    for device in ({"rows": above}, {"rows": below}, {"grp": ahead}, {"grp": behind}):
        pl.semaphore_signal(barrier, inc=1, device_id=device, device_id_type=MESH)
    pl.semaphore_wait(barrier, 4)

    def request(side):
        return pltpu.make_async_remote_copy(
            src_ref=reads_hbm,
            dst_ref=req_v.at[1 - side],
            send_sem=req_send.at[side],
            recv_sem=req_recv.at[1 - side],
            device_id={"rows": (below, above)[side]},
            device_id_type=MESH,
        )

    def reply(side):
        return pltpu.make_async_remote_copy(
            src_ref=stage.at[side],
            dst_ref=p_all.at[pl.ds(shard_rows + (1 - side) * cap, cap)],
            send_sem=rep_send.at[side],
            recv_sem=rep_recv.at[1 - side],
            device_id={"rows": (below, above)[side]},
            device_id_type=MESH,
        )

    for side in (0, 1):
        request(side).start()

    p_copy.wait()

    @pl.loop(0, shard_rows // 2, unroll=4)
    def _(pair):
        lanes = pl.ds(pl.multiple_of(pair * 128, 128), 128)
        p_turned[:, lanes] = p_loc[pl.ds(pair * 2, 2)].reshape(128, 128).T

    for side in (0, 1):
        request(side).wait()
    req_copy = pltpu.make_async_copy(req_v, req_s, local_sem.at[3])
    req_copy.start()
    req_copy.wait()
    for side in (0, 1):
        for c in range(cap):
            stage[side, c] = p_loc[jnp.maximum(req_s[side, 1 - side, c], 0)]
        reply(side).start()

    for copy in index_copies:
        copy.wait()

    @pl.loop(0, shard_rows // 2, unroll=4)
    def _(pair):
        lanes = pl.ds(pl.multiple_of(pair * 128, 128), 128)
        block = p_turned[:, lanes]
        owner = lane_pair(agg_ref[pair * 2], agg_ref[pair * 2 + 1], 16)
        for q in range(grp_count):
            keep = indicator(owner, q)
            p_masked[q, :, lanes] = block * jnp.concatenate([keep] * 8, axis=0)

    a_copy.wait()
    all_copy.wait()
    for side in (0, 1):
        reply(side).wait()

    def slot_sums(i, pair):
        columns = jnp.concatenate(
            [p_all[jnp.maximum(cols_ref[k, i], 0)] for k in range(slot_count)], axis=0
        )
        places = [
            jnp.where(cols_ref[k, i] >= 0, rap_ref[k, i], -1) for k in range(slot_count)
        ]
        spread = []
        for k in range(0, slot_count, 2):
            block = a_v[i, :, k * cells : (k + 2) * cells]
            place = lane_pair(places[k], places[k + 1], 16)
            keeps = [indicator(place, 2 * pair + h) for h in (0, 1)]
            spread.append(
                jnp.concatenate(
                    [block * jnp.concatenate([keep] * (cells // 16), axis=0) for keep in keeps],
                    axis=0,
                )
            )
        product = jnp.dot(
            jnp.concatenate(spread, axis=1), columns, preferred_element_type=jnp.float32
        ).astype(jnp.bfloat16)
        rows = pl.ds(pl.multiple_of(i * cells, cells), cells)
        for h in (0, 1):
            near[pair, rows, h * 128 : (h + 1) * 128] = product[h * cells : (h + 1) * cells]

    def quarter(pair):
        @pl.loop(0, shard_rows, unroll=min(8, shard_rows))
        def _(i):
            slot_sums(i, pair)

    def hop(way, step, pair):
        return pltpu.make_async_remote_copy(
            src_ref=outgoing.at[way, step, pair],
            dst_ref=incoming.at[way, step, pair],
            send_sem=ring_send.at[way, step, pair],
            recv_sem=ring_recv.at[way, step, pair],
            device_id={"grp": lax.rem(grp + 1 + way * (grp_count - 2), grp_count)},
            device_id_type=MESH,
        )

    def advance(pair, step, first=False, last=False):
        long = pair // 2
        turn = 1 - 2 * long
        far = lax.rem(grp + grp_count + turn * (half - step), grp_count)
        near_by = lax.rem(grp + grp_count - turn * (half - 1 - step), grp_count)
        left = jnp.concatenate([p_masked[far], p_masked[near_by]], axis=0)
        terms = jnp.dot(left, near[pair], preferred_element_type=jnp.float32)
        for side, way in ((0, long), (1, 1 - long)):
            own = last and side == 1
            if not first and not own:
                hop(way, step - 1, pair).wait_recv()
            for h in (0, 1):
                total = terms[side * 128 : (side + 1) * 128, h * 128 : (h + 1) * 128]
                if own:
                    total_v[pl.ds(pl.multiple_of((pair * 2 + h) * 128, 128), 128)] = total
                    continue
                if not first:
                    total = total + incoming[way, step - 1, pair, h].astype(jnp.float32)
                outgoing[way, step, pair, h] = total.astype(jnp.bfloat16)
            if not own:
                hop(way, step, pair).start()

    @pl.loop(0, 4)
    def _(pair):
        quarter(pair)
        advance(pair, 0, first=True)

        @pl.loop(1, jnp.minimum(pair, half - 2) + 1)
        def _(step):
            advance(pair - step, step)

    advance(0, half - 1, last=True)

    @pl.loop(1, 4)
    def _(pair):
        @pl.loop(pair, half - 1)
        def _(step):
            advance(3 - (step - pair), step)

        advance(pair, half - 1, last=True)

    @pl.loop(0, 4)
    def _(pair):
        long = pair // 2

        @pl.loop(0, half - 1)
        def _(step):
            hop(0, step, pair).wait_send()
            hop(1, step, pair).wait_send()

        hop(long, half - 1, pair).wait_recv()
        hop(1 - long, half - 2, pair).wait_recv()
        for h in (0, 1):
            rows = pl.ds(pl.multiple_of((pair * 2 + h) * 128, 128), 128)
            total_v[rows] = (
                total_v[rows]
                + incoming[long, half - 1, pair, h].astype(jnp.float32)
                + incoming[1 - long, half - 2, pair, h].astype(jnp.float32)
            )

    for d in range(128):
        out_ref[0, :, d * 128 : (d + 1) * 128] = total_v[pl.ds(d, CSLOT, stride=128)]

    for pair in range(4):
        hop(pair // 2, half - 1, pair).wait_send()


def on_device(row_count, grp_count, a_blocks, prolong, a_cols, read_slots, agg, rap_slot):
    shard_rows, cells, width = a_blocks.shape
    coarse = prolong.shape[2]
    cap = read_slots.shape[1]
    half = grp_count // 2
    vmem = pl.BlockSpec(memory_space=pltpu.VMEM)
    hbm = pl.BlockSpec(memory_space=pltpu.HBM)
    b16 = jnp.bfloat16
    dma = pltpu.SemaphoreType.DMA
    return pl.pallas_call(
        functools.partial(kernel, row_count, grp_count),
        out_shape=jax.ShapeDtypeStruct((1, CSLOT, coarse * coarse), jnp.float32),
        in_specs=[hbm] * 6,
        out_specs=vmem,
        scratch_shapes=[
            pltpu.SMEM(a_cols.shape[::-1], jnp.int32),
            pltpu.SMEM(agg.shape, jnp.int32),
            pltpu.SMEM(rap_slot.shape[::-1], jnp.int32),
            pltpu.VMEM((shard_rows, cells, width), b16),
            pltpu.VMEM((shard_rows, cells, coarse), b16),
            pltpu.VMEM((shard_rows + 2 * cap, cells, coarse), b16),
            pltpu.VMEM((coarse, shard_rows * cells), b16),
            pltpu.VMEM((grp_count, coarse, shard_rows * cells), b16),
            pltpu.VMEM((CSLOT // 2, shard_rows * cells, 2 * coarse), b16),
            pltpu.VMEM((CSLOT * coarse, coarse), jnp.float32),
            pltpu.VMEM((2, 2, cap), jnp.int32),
            pltpu.SMEM((2, 2, cap), jnp.int32),
            pltpu.VMEM((2, cap, cells, coarse), b16),
            pltpu.VMEM((2, half, 4, 2, coarse, coarse), b16),
            pltpu.VMEM((2, half, 4, 2, coarse, coarse), b16),
            dma((7,)),
            dma((2,)),
            dma((2,)),
            dma((2,)),
            dma((2,)),
            dma((2, half, 4)),
            dma((2, half, 4)),
        ],
        compiler_params=pltpu.CompilerParams(
            collective_id=0, has_side_effects=True, vmem_limit_bytes=56 * 1024 * 1024
        ),
    )(read_slots, a_cols.T, agg, rap_slot.T, a_blocks, prolong)

def solution(mesh):
    return jax.shard_map(
        functools.partial(on_device, mesh.shape["rows"], mesh.shape["grp"]),
        mesh=mesh,
        in_specs=(
            P(("rows", "grp"), None, None),
            P(("rows", "grp"), None, None),
            P(("rows", "grp"), None),
            P(("rows", "grp"), None),
            P(("rows", "grp")),
            P(("rows", "grp"), None),
        ),
        out_specs=P(("rows", "grp"), None, None),
        check_vma=False,
    )
```
